512 devices in a mesh: var: 16 (over z_lo, y), seq: 32 (over z_hi, x, core).
Axes of the slice: x: 4, y: 4, z: 16 (z_hi: 4, z_lo: 4; z = z_hi * 4 + z_lo), core: 2. Of those that a mesh axis runs over, the one named last changes fastest.
Arguments:
- pixels: bfloat16 [96, 4, 4096], P('var', None, 'seq'), may hold values from -6 to 6
- w_embed: bfloat16 [96, 4, 4096], P('var'), may hold values from -3 to 3
- var_embed: bfloat16 [96, 4096], P('var'), may hold values from -6 to 6
- var_mask: int32 [96], replicated, may hold values from 0 to 1, as said below
- agg_query: bfloat16 [4096], P('var')
- ln_gain: bfloat16 [4096], replicated, may hold values from 0.099609375 to 1.8984375
- w_up: bfloat16 [4096, 8192], P('seq', 'var'), may hold values from -0.09375 to 0.09375
- w_down: bfloat16 [8192, 4096], P('var', 'seq'), may hold values from -0.0625 to 0.0625
Outputs:
- mixed: bfloat16 [4096, 4096], P('seq', 'var')
The draws below stay inside these ranges and needn't reach their ends.
Inputs may be any that keep to these rules, and one draw needn't show every extreme that they name: `var_mask`: exactly 91 entries are 1, the others 0.
All inputs are finite; a program needn't handle non-finite values.
Results may differ from the reference program's by a relative error of at most 0.025.
Values may be sent and summed in bfloat16 or wider, within the bound.
A program may use at most 64 MiB of HBM per device.

```python
import math
import jax
import jax.numpy as jnp
from jax import lax

V = 96
PADDED = 5
PIX = 4
HEADS = 32
HS = 128
D = 4096
FF = 8192
TOK_DEV = 128
PATCHES = 4096
N_VAR = 16
N_SEQ = 32


def draw_var_mask(key, part):
    key = jax.random.fold_in(key, 1)
    order = jax.random.permutation(key, V)
    return (order >= PADDED).astype(jnp.int32)


def draw_agg_query(key, part):
    key = jax.random.fold_in(key, 2)
    base_key = jax.random.fold_in(key, 0)
    values = jax.random.normal(base_key, (HEADS, HS), jnp.float32)
    return values.reshape(HEADS * HS).astype(jnp.bfloat16)


def levels(key, extent, pieces, low, largest):
    def one(dim, blocks):
        draws = jax.random.uniform(jax.random.fold_in(jax.random.fold_in(key, 6), dim), (blocks,), jnp.float32, low / len(pieces), largest / len(pieces))
        return jnp.repeat(jnp.exp(draws), extent[dim] // blocks).reshape((-1,) + (1,) * (len(extent) - dim - 1))

    level = one(*pieces[0])
    for cut in pieces[1:]:
        level = level * one(*cut)
    return level


def gaussian(own_key, extent, scale, limit, cuts=(), dtype=jnp.bfloat16):
    drawn = jax.random.normal(own_key, extent, jnp.float32) * scale
    if len(cuts) > 0:
        drawn = levels(own_key, extent, cuts, -0.22, 0.18) * drawn
    return jnp.clip(drawn, min=-limit, max=limit).astype(dtype)


def setup_inputs(seed: int = 0) -> dict:
    keys = jax.random.split(jax.random.key(seed), 9)
    pixels = gaussian(keys[0], (V, PIX, PATCHES), 1.0, 6.0, ((0, 16), (2, 32)))
    w_embed = gaussian(keys[1], (V, PIX, D), PIX ** -0.5, 3.0, ((0, 16),))
    var_embed = gaussian(keys[2], (V, D), 1.0, 6.0, ((0, 16),))
    var_mask = draw_var_mask(jax.random.fold_in(keys[8], 71), 0)
    agg_query = draw_agg_query(jax.random.fold_in(keys[8], 71), 0)
    ln_gain = jnp.clip(1.0 + 0.18 * jax.random.normal(keys[5], (D,), jnp.float32), 0.099609375, 1.8984375).astype(jnp.bfloat16)
    w_up = gaussian(keys[6], (D, FF), D ** -0.5, 0.09375, ((0, 32), (1, 16)))
    w_down = gaussian(keys[7], (FF, D), FF ** -0.5, 0.0625, ((0, 16), (1, 32)))
    return {"pixels": pixels, "w_embed": w_embed, "var_embed": var_embed, "var_mask": var_mask, "agg_query": agg_query, "ln_gain": ln_gain, "w_up": w_up, "w_down": w_down}


def aggregate_block(pix_block, w_embed, var_embed, agg_query, var_mask):
    embedded = (jnp.einsum('vpt,vpc->vtc', pix_block.astype(jnp.float32), w_embed.astype(jnp.float32)) + var_embed.astype(jnp.float32)[:, None, :]).astype(jnp.bfloat16)
    count = pix_block.shape[2]
    parts = embedded.reshape(V, count, HEADS, HS).astype(jnp.float32)
    query = agg_query.reshape(HEADS, HS).astype(jnp.float32)
    scores = jnp.einsum('vthd,hd->vht', parts, query) / math.sqrt(HS)
    scores = jnp.where(var_mask[:, None, None] > 0, scores, -1e+30)
    top = lax.optimization_barrier(jnp.max(scores, axis=0, keepdims=True))
    expo = jnp.exp(scores - top)
    weights = (expo / lax.optimization_barrier(jnp.sum(expo, axis=0, keepdims=True))).astype(jnp.bfloat16)
    merged = jnp.einsum('vht,vthd->thd', weights.astype(jnp.float32), parts)
    return merged.reshape(count, HEADS * HS).astype(jnp.bfloat16)

def reference(pixels, w_embed, var_embed, var_mask, agg_query, ln_gain, w_up, w_down):
    blocks = pixels.reshape(V, PIX, N_SEQ, TOK_DEV).transpose(2, 0, 1, 3)
    aggregated = lax.map(lambda blk: aggregate_block(blk, w_embed, var_embed, agg_query, var_mask), blocks)
    aggregated = aggregated.reshape(N_SEQ * TOK_DEV, HEADS * HS)
    values = aggregated.astype(jnp.float32)
    mean = lax.optimization_barrier(jnp.mean(values, axis=1, keepdims=True))
    centered = values - mean
    variance = lax.optimization_barrier(jnp.mean(centered * centered, axis=1, keepdims=True))
    normed = (centered * lax.rsqrt(variance + 1e-05) * ln_gain.astype(jnp.float32)).astype(jnp.bfloat16)
    hidden = jax.nn.gelu(jnp.dot(normed, w_up, preferred_element_type=jnp.float32), approximate=True).astype(jnp.bfloat16)
    group = FF // N_VAR
    hidden_groups = hidden.reshape(hidden.shape[0], N_VAR, group).transpose(1, 0, 2)
    down_groups = w_down.reshape(N_VAR, group, HEADS * HS)

    def partial_term(pair):
        return jnp.dot(pair[0], pair[1], preferred_element_type=jnp.float32).astype(jnp.bfloat16).astype(jnp.float32)
    update = lax.optimization_barrier(jnp.sum(lax.map(partial_term, (hidden_groups, down_groups)), axis=0))
    return (values + update).astype(jnp.bfloat16)
```

```python
import math

import jax
import jax.numpy as jnp
from jax import lax
from jax.experimental import pallas as pl
from jax.experimental.pallas import tpu as pltpu
from jax.sharding import PartitionSpec as P

MESH = pl.DeviceIdType.MESH
F32, BF16 = jnp.float32, jnp.bfloat16
PIX, HS = 4, 128
N_VARS = 96
OWN_VARS = 6
ROWS = 32
DEPTH = 16 * ROWS
TOK, COLS, D, FF = 128, 256, 4096, 512
N_SEMS = 224


def block_of(iota):
    block, row = iota // ROWS, iota % ROWS
    owner = (block % 4) * 4 + block // 4
    local = jnp.where(row < OWN_VARS * PIX, row // PIX, row - OWN_VARS * PIX)
    return owner * OWN_VARS + local, row < OWN_VARS * (PIX + 1)


def kernel(
    pix_in, emb_in, bias_in, mask_in, query_in, gain_in, up_in, down_in, out,
    pix, emb, bias, mask, query, gain, rows_f, pix_f,
    tab_out, tab_mid, tab, pat, agg, norm, up, down, own_sum, term, got_y, got_z, part, total,
    local_sem, send_sem, recv_sem,
):
    var, seq = lax.axis_index("var"), lax.axis_index("seq")
    zl, y = var // 4, lax.rem(var, 4)
    zh, x, core = seq // 8, lax.rem(seq // 2, 4), lax.rem(seq, 2)
    z = zh * 4 + zl
    other = 1 - core

    def mod4(v):
        return lax.rem(v + 4, 4)

    def at_var(zl_, y_):
        return (zl_ * 4 + y_, seq)

    def at_seq(a, b, core_):
        return (var, mod4(zh + a) * 8 + mod4(x + b) * 2 + core_)

    def at_z(d):
        z_ = lax.rem(z + d + 16, 16)
        return (lax.rem(z_, 4) * 4 + y, (z_ // 4) * 8 + x * 2 + core)

    sibling = at_seq(0, 0, other)

    locals_ = []
    for i, (src, dst) in enumerate(
        (
            (pix_in, pix),
            (emb_in, emb),
            (bias_in, bias),
            (mask_in, mask),
            (query_in, query),
            (gain_in, gain),
            (up_in, up.at[zh, x * 2 + core]),
            (down_in, down.at[zh, x, :, pl.ds(pl.multiple_of(core * HS, HS), HS)]),
        )
    ):
        locals_.append(pltpu.make_async_copy(src, dst, local_sem.at[i]))
        locals_[-1].start()

    barrier = pltpu.get_barrier_semaphore()
    peers = [at_z(1), at_z(-1), at_z(2), at_z(-2), sibling]
    peers += [at_var(mod4(zl + i), y) for i in (1, 2, 3)]
    peers += [at_var(zl, mod4(y + i)) for i in (1, 2, 3)]
    peers += [at_seq(1, 0, core), at_seq(-1, 0, core), at_seq(0, 1, core), at_seq(0, -1, core)]
    for peer in peers:
        pl.semaphore_signal(barrier, inc=1, device_id=peer, device_id_type=MESH)

    sends, keys = [], {}

    def sem_of(key):
        return keys.setdefault(key, len(keys))

    def copy_of(src, dst, index, device):
        copy = pltpu.make_async_remote_copy(
            src_ref=src,
            dst_ref=dst,
            send_sem=send_sem.at[len(sends)],
            recv_sem=recv_sem.at[index],
            device_id=device,
            device_id_type=MESH,
        )
        return copy

    def send(src, dst, key, device):
        copy = copy_of(src, dst, sem_of(key), device)
        copy.start()
        sends.append(copy)

    def recv(dst, key):
        pltpu.make_async_remote_copy(
            src_ref=dst,
            dst_ref=dst,
            send_sem=send_sem.at[0],
            recv_sem=recv_sem.at[sem_of(key)],
            device_id=sibling,
            device_id_type=MESH,
        ).wait_recv()

    for i in range(3):
        locals_[i].wait()
    rows_f[:, OWN_VARS * (PIX + 1) :, :] = jnp.zeros((16, ROWS - OWN_VARS * (PIX + 1), HS), F32)
    for j in range(16):
        col = pl.ds(pl.multiple_of(j * COLS + core * HS, HS), HS)
        for v in range(OWN_VARS):
            rows_f[j, v * PIX : (v + 1) * PIX, :] = emb[v, :, col].astype(F32)
        rows_f[j, OWN_VARS * PIX : OWN_VARS * (PIX + 1), :] = bias[:, col].astype(F32)
    for j in range(16):
        tab_out[j // 4, j % 4] = rows_f[j].astype(BF16)
    row = lax.broadcasted_iota(jnp.int32, (ROWS, TOK), 0)
    pix_f[...] = jnp.where(row < OWN_VARS * (PIX + 1), 1.0, 0.0)
    for v in range(OWN_VARS):
        pix_f[v * PIX : (v + 1) * PIX, :] = pix[v].astype(F32)
    pat[y, zl] = pix_f[...].astype(BF16)

    pl.semaphore_wait(barrier, len(peers))

    for i in (1, 2, 3):
        send(pat.at[y, zl], pat.at[y, zl], ("pz", i), at_var(mod4(zl + i), y))
    for i, step in ((1, 1), (3, -1), (2, 2 - 4 * core)):
        send(tab_out.at[mod4(zl + i)], tab_mid.at[zl], ("tz", i), at_z(step))

    def part_of(m, a, b, core_, half):
        if m == 0:
            ref = up.at[mod4(zh + a), mod4(x + b) * 2 + core_]
            return ref if half is None else ref.at[pl.ds(half * 64, 64)]
        rows = pl.ds(0, FF) if half is None else pl.ds(half * 256, 256)
        cols = pl.ds(pl.multiple_of(core_ * HS, HS), HS)
        return down.at[mod4(zh + a), mod4(x + b), rows, cols]

    def weight(m, a, b, half, way):
        da, db = {"z+": (1, 0), "z-": (-1, 0), "x+": (0, 1), "x-": (0, -1), "s": (0, 0)}[way]
        place = part_of(m, a, b, core, half)
        src = place
        if a == 0 and b == 0:
            src = (up_in, down_in)[m]
            if half is not None:
                src = src.at[pl.ds(half * (64, 256)[m], (64, 256)[m])]
        key = ("w", m, (a - da) % 4, (b - db) % 4, way == "s", half)
        send(src, place, key, at_seq(da, db, other if way == "s" else core))

    def weight_here(m, a, b, half=None, swapped=False):
        recv(part_of(m, a, b, other if swapped else core, half), ("w", m, a % 4, b % 4, swapped, half))

    def first(m):
        weight(m, 0, 0, 0, "z+")
        weight(m, 0, 0, 1, "z-")
        weight(m, 0, 0, 1, "z+")
        weight(m, 0, 0, 0, "z-")
        spread(m, 0)

    def spread(m, a):
        weight(m, a, 0, None, "x+")
        weight(m, a, 0, None, "x-")
        weight(m, a, 0, None, "s")

    def x_near(m, a):
        weight_here(m, a, -1)
        weight(m, a, -1, 0, "x+")
        weight(m, a, -1, None, "s")
        weight_here(m, a, 1)
        weight(m, a, 1, 1, "x-")
        weight(m, a, 1, None, "s")

    def x_far(m, a):
        weight_here(m, a, 2, 0)
        weight_here(m, a, 2, 1)
        weight(m, a, 2, None, "s")

    def z_near(m):
        weight_here(m, -1, 0, 0)
        weight(m, -1, 0, 0, "z+")
        weight_here(m, 1, 0, 1)
        weight(m, 1, 0, 1, "z-")

    def z_near_rest(m):
        weight_here(m, -1, 0, 1)
        spread(m, -1)
        weight_here(m, 1, 0, 0)
        spread(m, 1)

    def z_far(m):
        weight_here(m, 2, 0, 0)
        weight_here(m, 2, 0, 1)
        spread(m, 2)

    def swapped(m, a):
        for b in range(4):
            weight_here(m, a, b, None, True)

    first(0)
    tab_mid[zl] = tab_out[zl]

    for i in (1, 2, 3):
        recv(pat.at[y, mod4(zl - i)], ("pz", i))
    for i in (1, 2, 3):
        send(pat.at[y], pat.at[y], ("py", i), at_var(zl, mod4(y + i)))
    for i in (1, 2, 3):
        recv(tab_mid.at[mod4(zl - i)], ("tz", i))
    for i in (1, 2, 3):
        y_ = mod4(y + i)
        send(tab_mid.at[:, y_], tab.at[core, y], ("ty", i), at_var(zl, y_))
    tab[core, y] = tab_mid[:, y]
    for i in (1, 2, 3):
        recv(tab.at[core, mod4(y - i)], ("ty", i))
    send(tab.at[core], tab.at[core], "ts", sibling)
    for i in (1, 2, 3):
        recv(pat.at[mod4(y - i)], ("py", i))
    recv(tab.at[other], "ts")

    locals_[3].wait()
    locals_[4].wait()
    points = pat[...].reshape(DEPTH, TOK)
    points_f = points.astype(F32)
    twice = jnp.concatenate([points_f, points_f], axis=1)
    query_f = query[...].astype(F32).reshape(1, COLS)
    tables = [tab[h].reshape(DEPTH, HS) for h in range(2)]
    shares = []
    for h in range(2):
        dots = jnp.sum(tables[h].astype(F32) * query_f[:, h * HS : (h + 1) * HS], axis=1, keepdims=True)
        shares.append((dots * (1.0 / math.sqrt(HS))) * points_f)
    share = jnp.concatenate(shares, axis=1)
    which, real = block_of(lax.broadcasted_iota(jnp.int32, (N_VARS, DEPTH), 1))
    collect = jnp.where(
        (which == lax.broadcasted_iota(jnp.int32, (N_VARS, DEPTH), 0)) & real, 1.0, 0.0
    ).astype(BF16)
    scores = jnp.zeros((N_VARS, COLS), F32)
    for _ in range(3):
        piece = share.astype(BF16)
        share = share - piece.astype(F32)
        scores = scores + jnp.dot(collect, piece, preferred_element_type=F32)
    diagonal = lax.broadcasted_iota(jnp.int32, (N_VARS, N_VARS), 0) == lax.broadcasted_iota(
        jnp.int32, (N_VARS, N_VARS), 1
    )
    keep = jnp.sum(
        jnp.where(diagonal, mask[...].astype(F32).reshape(1, N_VARS), 0.0), axis=1, keepdims=True
    )
    scores = jnp.where(keep > 0.0, scores, -1e30)
    expo = jnp.exp(scores - jnp.max(scores, axis=0, keepdims=True))
    weights = (expo / jnp.sum(expo, axis=0, keepdims=True)).astype(BF16)
    which, real = block_of(lax.broadcasted_iota(jnp.int32, (DEPTH, N_VARS), 0))
    expand = jnp.where(
        (which == lax.broadcasted_iota(jnp.int32, (DEPTH, N_VARS), 1)) & real, 1.0, 0.0
    ).astype(BF16)
    mixed = jnp.dot(expand, weights, preferred_element_type=F32) * twice
    high = mixed.astype(BF16)
    low = (mixed - high.astype(F32)).astype(BF16)
    over_rows = (((0,), (0,)), ((), ()))
    merged = []
    for h in range(2):
        cols = slice(h * HS, (h + 1) * HS)
        merged.append(
            lax.dot_general(high[:, cols], tables[h], over_rows, preferred_element_type=F32)
            + lax.dot_general(low[:, cols], tables[h], over_rows, preferred_element_type=F32)
        )
    agg[var] = jnp.concatenate(merged, axis=1).astype(BF16)

    for i in (1, 2, 3):
        send(agg.at[var], agg.at[var], ("az", i), at_var(mod4(zl + i), y))
    for i in (1, 3, 2):
        send(agg.at[var], agg.at[var], ("ay", 0, i), at_var(zl, mod4(y + i)))
    x_near(0, 0)
    z_near(0)
    first(1)
    for j in (1, 2, 3):
        place = agg.at[mod4(zl - j) * 4 + y]
        recv(place, ("az", j))
        for i in (1, 3, 2):
            send(place, place, ("ay", j, i), at_var(zl, mod4(y + i)))
    z_near_rest(0)
    x_far(0, 0)
    x_near(1, 0)
    for j in range(4):
        for i in (1, 3, 2):
            recv(agg.at[mod4(zl - j) * 4 + mod4(y - i)], ("ay", j, i))

    def row_sum(v, acc):
        return acc + jnp.sum(agg[v].astype(F32), axis=1, keepdims=True)

    mean = lax.fori_loop(0, 16, row_sum, jnp.zeros((TOK, 1), F32)) * (1.0 / D)

    def square_sum(v, acc):
        centered = agg[v].astype(F32) - mean
        return acc + jnp.sum(centered * centered, axis=1, keepdims=True)

    variance = lax.fori_loop(0, 16, square_sum, jnp.zeros((TOK, 1), F32)) * (1.0 / D)
    scale = lax.rsqrt(variance + 1e-05)
    locals_[5].wait()
    for v in range(16):
        cols = slice(v * COLS, (v + 1) * COLS)
        gains = gain[cols].astype(F32).reshape(1, COLS)
        norm[v // 4, :, (v % 4) * COLS : (v % 4 + 1) * COLS] = (
            (agg[v].astype(F32) - mean) * scale * gains
        ).astype(BF16)

    x_near(0, -1)
    x_near(0, 1)
    z_far(0)
    x_far(0, -1)
    x_far(0, 1)
    z_near(1)
    x_near(0, 2)
    x_far(1, 0)

    locals_[6].wait()

    def up_part(a):
        swapped(0, a)
        q = mod4(zh + a)
        return jnp.dot(norm[q], up[q].reshape(1024, FF), preferred_element_type=F32)

    part[...] = up_part(0)
    part[...] += up_part(-1)
    part[...] += up_part(1)
    x_far(0, 2)
    z_near_rest(1)
    hidden = jax.nn.gelu(part[...] + up_part(2), approximate=True).astype(BF16)

    def down_part(a):
        q = mod4(zh + a)
        swapped(1, a)
        for i in (2, 1, 3, 0):
            y_ = mod4(y + i)
            value = jnp.dot(hidden, down[q, y_], preferred_element_type=F32)
            if i == 0:
                own_sum[a % 4] = value
            else:
                term[a % 4, i] = value.astype(BF16)
                send(term.at[a % 4, i], got_y.at[a % 4, i], ("ry", a % 4, i), at_var(zl, y_))

    optional = []

    def down_sum(a):
        a = a % 4
        q = mod4(zh + a)
        value = own_sum[a]
        for i in (1, 2, 3):
            recv(got_y.at[a, i], ("ry", a, i))
            value = value + got_y[a, i].astype(F32)
        mine = zl == q
        away = mod4(zl - q)
        base = sem_of(("rz", 1))
        assert [sem_of(("rz", i)) for i in (1, 2, 3)] == [base, base + 1, base + 2]

        @pl.when(mine)
        def _():
            total[...] = value

        copy = copy_of(
            own_bf.at[a], got_z.at[away], base + lax.rem(away + 2, 3), at_var(q, y)
        )
        sends.append(None)

        @pl.when(jnp.logical_not(mine))
        def _():
            own_bf[a] = value.astype(BF16)
            copy.start()

        optional.append((mine, copy))

    own_bf = term.at[:, 0]
    locals_[7].wait()
    down_part(0)
    x_near(1, -1)
    x_near(1, 1)
    down_sum(0)
    z_far(1)
    x_far(1, -1)
    x_far(1, 1)
    down_part(-1)
    down_part(1)
    x_near(1, 2)
    down_sum(-1)
    down_sum(1)
    x_far(1, 2)
    down_part(2)
    for copy in sends:
        if copy is not None:
            copy.wait_send()
    down_sum(2)
    result = agg[var].astype(F32) + total[...]
    for i in (1, 2, 3):
        recv(got_z.at[i], ("rz", i))
        result = result + got_z[i].astype(F32)
    out[...] = result.astype(BF16)
    for mine, copy in optional:
        @pl.when(jnp.logical_not(mine))
        def _(copy=copy):
            copy.wait_send()
    assert len(keys) <= N_SEMS and len(sends) <= N_SEMS


def shards(pixels, w_embed, var_embed, var_mask, agg_query, ln_gain, w_up, w_down):
    vmem = pltpu.VMEM
    return pl.pallas_call(
        kernel,
        out_shape=jax.ShapeDtypeStruct((TOK, COLS), BF16),
        in_specs=[pl.BlockSpec(memory_space=pl.ANY)] * 8,
        out_specs=pl.BlockSpec(memory_space=pltpu.VMEM),
        scratch_shapes=[
            vmem((OWN_VARS, PIX, TOK), BF16),
            vmem((OWN_VARS, PIX, D), BF16),
            vmem((OWN_VARS, D), BF16),
            vmem((N_VARS,), jnp.int32),
            vmem((COLS,), BF16),
            vmem((D,), BF16),
            vmem((16, ROWS, HS), F32),
            vmem((ROWS, TOK), F32),
            vmem((4, 4, ROWS, HS), BF16),
            vmem((4, 4, ROWS, HS), BF16),
            vmem((2, 4, 4, ROWS, HS), BF16),
            vmem((4, 4, ROWS, TOK), BF16),
            vmem((16, TOK, COLS), BF16),
            vmem((4, TOK, 1024), BF16),
            vmem((4, 8, 128, FF), BF16),
            vmem((4, 4, FF, COLS), BF16),
            vmem((4, TOK, COLS), F32),
            vmem((4, 4, TOK, COLS), BF16),
            vmem((4, 4, TOK, COLS), BF16),
            vmem((4, TOK, COLS), BF16),
            vmem((TOK, FF), F32),
            vmem((TOK, COLS), F32),
            pltpu.SemaphoreType.DMA((8,)),
            pltpu.SemaphoreType.DMA((N_SEMS,)),
            pltpu.SemaphoreType.DMA((N_SEMS,)),
        ],
        compiler_params=pltpu.CompilerParams(
            collective_id=0, has_side_effects=True, vmem_limit_bytes=56 * 1024 * 1024
        ),
    )(pixels, w_embed, var_embed, var_mask, agg_query, ln_gain, w_up, w_down)


def solution(mesh):
    return jax.shard_map(
        shards,
        mesh=mesh,
        in_specs=(
            P("var", None, "seq"),
            P("var", None, None),
            P("var", None),
            P(),
            P("var"),
            P(),
            P("seq", "var"),
            P("var", "seq"),
        ),
        out_specs=P("seq", "var"),
        check_vma=False,
    )
```

```python
import math

import jax
import jax.numpy as jnp
from jax import lax
from jax.experimental import pallas as pl
from jax.experimental.pallas import tpu as pltpu
from jax.sharding import PartitionSpec as P

MESH = pl.DeviceIdType.MESH
F32, BF16 = jnp.float32, jnp.bfloat16
PIX, HS = 4, 128
N_VARS = 96
OWN_VARS = 6
ROWS = 32
DEPTH = 16 * ROWS
TOK, COLS, D, FF = 128, 256, 4096, 512
N_SENT, N_RECV = 14, 120
SPLIT = (2, 2)
SPLIT_NEAR = (2, 2)
ORDER = (
    ("start",), ("x0", 0), ("x0", 1), ("py",), ("X", 0, 0, -1, 0), ("X", 0, 0, 1, 1), ("ty",), ("XR", 0, 0, -1),
    ("XR", 0, 0, 1), ("X", 1, 0, -1, 0), ("X", 1, 0, 1, 1), ("XR", 1, 0, -1), ("XR", 1, 0, 1), ("ts",),
    ("XR", 0, 0, 2), ("agg",), ("Z", 0, -1, 0), ("Z", 0, 1, 1), ("z1",), ("XR", 1, 0, 2), ("X", 0, -1, -1, 0),
    ("Z", 0, -1, 1), ("S", 0, -1, 0), ("Z", 0, 1, 0), ("S", 0, 1, 0), ("ayz", 1), ("X", 0, 1, 1, 1), ("ayz", 2),
    ("X", 0, -1, 1, 1), ("XR", 0, -1, 1), ("XR", 0, -1, -1), ("XR", 0, 1, 1), ("ayz", 3), ("X", 0, 1, -1, 0),
    ("XR", 0, 1, -1), ("XR", 0, -1, 2), ("XR", 0, 1, 2), ("Z", 0, 2, 0), ("Z", 0, 2, 1), ("S", 0, 2, 0), ("ln",),
    ("up", 0), ("up", -1), ("up", 1), ("X", 0, 2, -1, 0), ("XR", 0, 2, -1), ("X", 0, 2, 1, 1), ("XR", 0, 2, 1),
    ("Z", 1, -1, 0), ("Z", 1, 1, 1), ("XR", 0, 2, 2), ("X", 1, -1, -1, 0), ("up", 2), ("hid",), ("dp", 0, 0),
    ("Z", 1, -1, 1), ("S", 1, -1, 0), ("Z", 1, 1, 0), ("S", 1, 1, 0), ("dp", 0, -1), ("X", 1, 1, 1, 1), ("dp", 0, 1),
    ("dp", 0, 2), ("dp", -1, 0), ("dp", 1, 0), ("XR", 1, -1, -1), ("X", 1, -1, 1, 1), ("XR", 1, -1, 1),
    ("dp", -1, -1), ("dp", -1, 1), ("Z", 1, 2, 0), ("Z", 1, 2, 1), ("S", 1, 2, 0), ("X", 1, 1, -1, 0),
    ("XR", 1, 1, -1), ("XR", 1, 1, 1), ("ds", 0), ("dp", 2, 0), ("dp", 1, -1), ("dp", 1, 1), ("XR", 1, -1, 2),
    ("X", 1, 2, -1, 0), ("dp", -1, 2), ("XR", 1, 2, -1), ("X", 1, 2, 1, 1), ("XR", 1, 2, 1), ("dp", 2, -1),
    ("XR", 1, 1, 2), ("dp", 2, 1), ("ds", -1), ("dp", 1, 2), ("XR", 1, 2, 2), ("sent",), ("dp", 2, 2), ("ds", 1),
    ("ds", 2), ("fin",),
)


def block_of(iota):
    block, row = iota // ROWS, iota % ROWS
    owner = (block % 4) * 4 + block // 4
    local = jnp.where(row < OWN_VARS * PIX, row // PIX, row - OWN_VARS * PIX)
    return owner * OWN_VARS + local, row < OWN_VARS * (PIX + 1)


def kernel(
    pix_in, emb_in, bias_in, mask_in, query_in, gain_in, up_in, down_in, out,
    pix, emb, bias, mask, query, gain, rows_f, pix_f,
    tab_out, tab_mid, tab, pat, agg, norm, up, down, own_sum, term, got_y, got_z, summed, hidden_ref, part, total,
    local_sem, send_sem, recv_sem,
):
    var, seq = lax.axis_index("var"), lax.axis_index("seq")
    zl, y = var // 4, lax.rem(var, 4)
    zh, x, core = seq // 8, lax.rem(seq // 2, 4), lax.rem(seq, 2)
    z = zh * 4 + zl
    other = 1 - core

    def mod4(v):
        return lax.rem(v + 4, 4)

    def at_var(zl_, y_):
        return (zl_ * 4 + y_, seq)

    def at_seq(a, b, core_):
        return (var, mod4(zh + a) * 8 + mod4(x + b) * 2 + core_)

    def at_z(d):
        z_ = lax.rem(z + d + 16, 16)
        return (lax.rem(z_, 4) * 4 + y, (z_ // 4) * 8 + x * 2 + core)

    sibling = at_seq(0, 0, other)

    locals_ = []
    for i, (src, dst) in enumerate(
        (
            (pix_in, pix),
            (emb_in, emb),
            (bias_in, bias),
            (mask_in, mask),
            (query_in, query),
            (gain_in, gain),
            (up_in, up.at[zh, x, core]),
            (down_in, down.at[zh, x, :, pl.ds(pl.multiple_of(core * HS, HS), HS)]),
        )
    ):
        locals_.append(pltpu.make_async_copy(src, dst, local_sem.at[i]))
        locals_[-1].start()

    barrier = pltpu.get_barrier_semaphore()
    peers = [at_z(1), at_z(-1), at_z(2), at_z(-2), sibling]
    peers += [at_var(mod4(zl + i), y) for i in (1, 2, 3)]
    peers += [at_var(zl, mod4(y + i)) for i in (1, 2, 3)]
    peers += [at_seq(1, 0, core), at_seq(-1, 0, core), at_seq(0, 1, core), at_seq(0, -1, core)]
    for peer in peers:
        pl.semaphore_signal(barrier, inc=1, device_id=peer, device_id_type=MESH)

    groups, keys = {}, {}

    def sem_of(key):
        return keys.setdefault(key, len(keys))

    def copy_of(src, dst, group, key, device):
        return pltpu.make_async_remote_copy(
            src_ref=src,
            dst_ref=dst,
            send_sem=send_sem.at[groups.setdefault(group, len(groups))],
            recv_sem=recv_sem.at[sem_of(key)],
            device_id=device,
            device_id_type=MESH,
        )

    def send(src, dst, group, key, device):
        copy_of(src, dst, group, key, device).start()

    def recv(view, key):
        copy_of(view, view, next(iter(groups)), key, sibling).wait_recv()

    def sent(view, group):
        copy_of(view, view, group, next(iter(keys)), sibling).wait_send()

    for i in range(3):
        locals_[i].wait()
    rows_f[:, OWN_VARS * (PIX + 1) :, :] = jnp.zeros((16, ROWS - OWN_VARS * (PIX + 1), HS), F32)
    for j in range(16):
        col = pl.ds(pl.multiple_of(j * COLS + core * HS, HS), HS)
        for v in range(OWN_VARS):
            rows_f[j, v * PIX : (v + 1) * PIX, :] = emb[v, :, col].astype(F32)
        rows_f[j, OWN_VARS * PIX : OWN_VARS * (PIX + 1), :] = bias[:, col].astype(F32)
    for j in range(16):
        tab_out[j // 4, j % 4] = rows_f[j].astype(BF16)
    row = lax.broadcasted_iota(jnp.int32, (ROWS, TOK), 0)
    pix_f[...] = jnp.where(row < OWN_VARS * (PIX + 1), 1.0, 0.0)
    for v in range(OWN_VARS):
        pix_f[v * PIX : (v + 1) * PIX, :] = pix[v].astype(F32)
    pat[y, zl] = pix_f[...].astype(BF16)

    pl.semaphore_wait(barrier, len(peers))


    def pieces(m, a):
        return (SPLIT if a % 4 else SPLIT_NEAR)[m]

    def rows_of(m, a, p, count=1):
        n = (HS, FF)[m] // pieces(m, a)
        return pl.ds(p * n, n * count)

    def block(m, a, b, core_):
        if m == 0:
            return up.at[mod4(zh + a), mod4(x + b), core_]
        return down.at[mod4(zh + a), mod4(x + b), :, pl.ds(pl.multiple_of(core_ * HS, HS), HS)]

    def piece(m, a, b, p, count=1):
        if m == 0:
            return block(m, a, b, core).at[rows_of(m, a, p, count)]
        cols = pl.ds(pl.multiple_of(core * HS, HS), HS)
        return down.at[mod4(zh + a), mod4(x + b), rows_of(m, a, p, count), cols]

    def z_key(m, a, p):
        return ("z", m, a % 4, p)

    def x_key(m, a, b, p):
        n = pieces(m, a)
        alone = (b % 4 == 3 and p < n // 2) or (b % 4 == 1 and p >= n // 2)
        return ("x", m, a % 4, b % 4, p if alone else "rest")

    def z_send(m, a, p, way):
        step = {"z+": 1, "z-": -1}[way]
        if a == 0:
            rows = rows_of(m, 1, p)
            src = (up_in, down_in)[m].at[rows]
            if m == 0:
                dst = up.at[zh, x, core].at[rows]
            else:
                dst = down.at[zh, x, rows, pl.ds(pl.multiple_of(core * HS, HS), HS)]
        else:
            src = dst = piece(m, a, 0, p)
        send(src, dst, ("z", m), z_key(m, a - step, p), at_seq(step, 0, core))

    def x_send(m, a, b, p, way):
        step = {"x+": 1, "x-": -1}[way]
        src = dst = piece(m, a, b, p)
        if a == 0 and b == 0:
            src = (up_in, down_in)[m].at[rows_of(m, 0, p)]
        send(src, dst, ("x", m), x_key(m, a, b - step, p), at_seq(0, step, core))

    def s_key(m, a, b):
        return ("s", m, a % 4, b % 4 if m == 1 and a else 0)

    def swap(m, a, b):
        place = block(m, a, b, core)
        src = (up_in, down_in)[m] if a == 0 and b == 0 else place
        send(src, place, ("s", m), s_key(m, a, b), sibling)

    def z_first(m):
        n = pieces(m, 1)
        for i in range(n):
            z_send(m, 0, i, "z+")
            z_send(m, 0, n - 1 - i, "z-")

    def x_first(m):
        n = pieces(m, 0)
        for i in range(n):
            x_send(m, 0, 0, i, "x+")
            x_send(m, 0, 0, n - 1 - i, "x-")
        swap(m, 0, 0)

    def z_piece(m, a, p):
        n = pieces(m, a)
        recv(piece(m, a, 0, p), z_key(m, a, p))
        if a == -1 and p < n // 2:
            z_send(m, a, p, "z+")
        if a == 1 and p >= n // 2:
            z_send(m, a, p, "z-")
        x_send(m, a, 0, p, "x+")
        x_send(m, a, 0, p, "x-")

    def x_piece(m, a, b, p):
        recv(piece(m, a, b, p), x_key(m, a, b, p))
        x_send(m, a, b, p, "x+" if b == -1 else "x-")

    def x_rest(m, a, b):
        n = pieces(m, a)
        first, count = {-1: (n // 2, n // 2), 1: (0, n // 2), 2: (0, n)}[b]
        recv(piece(m, a, b, first, count), x_key(m, a, b, first))
        swap(m, a, b)

    def start():
        for i in (1, 2, 3):
            send(pat.at[y, zl], pat.at[y, zl], "pz", "pz", at_var(mod4(zl + i), y))
        for i, step in ((1, 1), (3, -1), (2, 2 - 4 * core)):
            send(tab_out.at[mod4(zl + i)], tab_mid.at[zl], "tz", "tz", at_z(step))
        z_first(0)
        tab_mid[zl] = tab_out[zl]

    def points_y():
        recv(pat.at[0, 0:3], "pz")
        for i in (1, 2, 3):
            send(pat.at[y], pat.at[y], "py", "py", at_var(zl, mod4(y + i)))

    def table_y():
        recv(tab_mid.at[0:3], "tz")
        for i in (1, 2, 3):
            y_ = mod4(y + i)
            send(tab_mid.at[:, y_], tab.at[core, y], "ty", "ty", at_var(zl, y_))
        tab[core, y] = tab_mid[:, y]

    def table_swap():
        recv(tab.at[core, 0:3], "ty")
        send(tab.at[core], tab.at[core], "ts", "ts", sibling)

    def aggregate():
        recv(pat.at[0:3], "py")
        recv(tab.at[other], "ts")
        locals_[3].wait()
        locals_[4].wait()
        points = pat[...].reshape(DEPTH, TOK)
        points_f = points.astype(F32)
        twice = jnp.concatenate([points_f, points_f], axis=1)
        query_f = query[...].astype(F32).reshape(1, COLS)
        tables = [tab[h].reshape(DEPTH, HS) for h in range(2)]
        shares = []
        for h in range(2):
            dots = jnp.sum(tables[h].astype(F32) * query_f[:, h * HS : (h + 1) * HS], axis=1, keepdims=True)
            shares.append((dots * (1.0 / math.sqrt(HS))) * points_f)
        share = jnp.concatenate(shares, axis=1)
        which, real = block_of(lax.broadcasted_iota(jnp.int32, (N_VARS, DEPTH), 1))
        collect = jnp.where(
            (which == lax.broadcasted_iota(jnp.int32, (N_VARS, DEPTH), 0)) & real, 1.0, 0.0
        ).astype(BF16)
        scores = jnp.zeros((N_VARS, COLS), F32)
        for _ in range(3):
            piece = share.astype(BF16)
            share = share - piece.astype(F32)
            scores = scores + jnp.dot(collect, piece, preferred_element_type=F32)
        diagonal = lax.broadcasted_iota(jnp.int32, (N_VARS, N_VARS), 0) == lax.broadcasted_iota(
            jnp.int32, (N_VARS, N_VARS), 1
        )
        keep = jnp.sum(
            jnp.where(diagonal, mask[...].astype(F32).reshape(1, N_VARS), 0.0), axis=1, keepdims=True
        )
        scores = jnp.where(keep > 0.0, scores, -1e30)
        expo = jnp.exp(scores - jnp.max(scores, axis=0, keepdims=True))
        weights = (expo / jnp.sum(expo, axis=0, keepdims=True)).astype(BF16)
        which, real = block_of(lax.broadcasted_iota(jnp.int32, (DEPTH, N_VARS), 0))
        expand = jnp.where(
            (which == lax.broadcasted_iota(jnp.int32, (DEPTH, N_VARS), 1)) & real, 1.0, 0.0
        ).astype(BF16)
        mixed = jnp.dot(expand, weights, preferred_element_type=F32) * twice
        high = mixed.astype(BF16)
        low = (mixed - high.astype(F32)).astype(BF16)
        over_rows = (((0,), (0,)), ((), ()))
        merged = []
        for h in range(2):
            cols = slice(h * HS, (h + 1) * HS)
            merged.append(
                lax.dot_general(high[:, cols], tables[h], over_rows, preferred_element_type=F32)
                + lax.dot_general(low[:, cols], tables[h], over_rows, preferred_element_type=F32)
            )
        agg[var] = jnp.concatenate(merged, axis=1).astype(BF16)

        for i in (1, 2, 3):
            send(agg.at[var], agg.at[var], "agg", ("az", i), at_var(mod4(zl + i), y))
        for i in (1, 3, 2):
            send(agg.at[var], agg.at[var], "agg", "ay", at_var(zl, mod4(y + i)))

    def features_y(j):
        place = agg.at[mod4(zl - j) * 4 + y]
        recv(place, ("az", j))
        for i in (1, 3, 2):
            send(place, place, "agg", "ay", at_var(zl, mod4(y + i)))

    def layer_norm():
        recv(agg.at[0:12], "ay")
        sums = jnp.zeros((TOK, COLS), F32)
        for v in range(16):
            sums = sums + agg[v].astype(F32)
        mean = jnp.sum(sums, axis=1, keepdims=True) * (1.0 / D)
        sums = jnp.zeros((TOK, COLS), F32)
        for v in range(16):
            centered = agg[v].astype(F32) - mean
            sums = sums + centered * centered
        variance = jnp.sum(sums, axis=1, keepdims=True) * (1.0 / D)
        scale = lax.rsqrt(variance + 1e-05)
        locals_[5].wait()
        for v in range(16):
            cols = slice(v * COLS, (v + 1) * COLS)
            gains = gain[cols].astype(F32).reshape(1, COLS)
            norm[v // 4, :, (v % 4) * COLS : (v % 4 + 1) * COLS] = (
                (agg[v].astype(F32) - mean) * scale * gains
            ).astype(BF16)

    def up_part(a):
        if a == 0:
            locals_[6].wait()
        q = mod4(zh + a)
        recv(up.at[q, :, other], s_key(0, a, 0))
        value = jnp.dot(norm[q], up[q].reshape(1024, FF), preferred_element_type=F32)
        part[...] = value if a == 0 else part[...] + value

    def activate():
        hidden_ref[...] = jax.nn.gelu(part[...], approximate=True).astype(BF16)

    def down_part(a, b):
        if a == 0 and b == 0:
            locals_[7].wait()
        q, y_ = mod4(zh + a), mod4(x + b)
        cols = pl.ds(pl.multiple_of(other * HS, HS), HS)
        if a:
            recv(down.at[q, y_, :, cols], s_key(1, a, b))
        elif b == 0:
            recv(down.at[q, :, :, cols], s_key(1, a, b))
        value = jnp.dot(hidden_ref[...], down[q, y_], preferred_element_type=F32)
        away = mod4(y_ - y)

        @pl.when(away == 0)
        def _():
            own_sum[a % 4] = value

        term[a % 4, b % 4] = value.astype(BF16)

        @pl.when(away != 0)
        def _():
            send(term.at[a % 4, b % 4], got_y.at[a % 4, away], "ry", ("ry", a % 4), at_var(zl, y_))

    def down_sum(a):
        a = a % 4
        q = mod4(zh + a)
        recv(got_y.at[a, 1:4], ("ry", a))
        value = own_sum[a]
        for i in (1, 2, 3):
            value = value + got_y[a, i].astype(F32)
        away = mod4(zl - q)

        @pl.when(away == 0)
        def _():
            total[...] = value

        summed[a] = value.astype(BF16)

        @pl.when(away != 0)
        def _():
            send(summed.at[a], got_z.at[away], "rz", "rz", at_var(q, y))

    def all_sent():
        for m in (0, 1):
            sent(up.at[0, 0:3, 0], ("z", m))
            sent(up.at[0:3, :, 0], ("x", m))
            sent(up.at[0:2], ("s", m))
        sent(pat.at[0, 0:3], "pz")
        sent(pat.at[0:3], "py")
        sent(tab_mid.at[0:3], "tz")
        sent(tab_mid.at[0:3], "ty")
        sent(tab.at[0], "ts")
        sent(agg.at[0:15], "agg")

    def finish():
        result = agg[var].astype(F32) + total[...]
        recv(got_z.at[1:4], "rz")
        for i in (1, 2, 3):
            result = result + got_z[i].astype(F32)
        out[...] = result.astype(BF16)
        sent(got_y.at[0:3], "ry")
        sent(got_z.at[0:3], "rz")

    steps = {
        "start": start,
        "x0": x_first,
        "z1": lambda: z_first(1),
        "Z": z_piece,
        "X": x_piece,
        "XR": x_rest,
        "S": swap,
        "py": points_y,
        "ty": table_y,
        "ts": table_swap,
        "agg": aggregate,
        "ayz": features_y,
        "ln": layer_norm,
        "up": up_part,
        "hid": activate,
        "dp": down_part,
        "sent": all_sent,
        "ds": down_sum,
        "fin": finish,
    }
    for name, *rest in ORDER:
        steps[name](*rest)
    assert len(keys) <= N_RECV and len(groups) <= N_SENT


def shards(pixels, w_embed, var_embed, var_mask, agg_query, ln_gain, w_up, w_down):
    vmem = pltpu.VMEM
    return pl.pallas_call(
        kernel,
        out_shape=jax.ShapeDtypeStruct((TOK, COLS), BF16),
        in_specs=[pl.BlockSpec(memory_space=pl.ANY)] * 8,
        out_specs=pl.BlockSpec(memory_space=pltpu.VMEM),
        scratch_shapes=[
            vmem((OWN_VARS, PIX, TOK), BF16),
            vmem((OWN_VARS, PIX, D), BF16),
            vmem((OWN_VARS, D), BF16),
            vmem((N_VARS,), jnp.int32),
            vmem((COLS,), BF16),
            vmem((D,), BF16),
            vmem((16, ROWS, HS), F32),
            vmem((ROWS, TOK), F32),
            vmem((4, 4, ROWS, HS), BF16),
            vmem((4, 4, ROWS, HS), BF16),
            vmem((2, 4, 4, ROWS, HS), BF16),
            vmem((4, 4, ROWS, TOK), BF16),
            vmem((16, TOK, COLS), BF16),
            vmem((4, TOK, 1024), BF16),
            vmem((4, 4, 2, 128, FF), BF16),
            vmem((4, 4, FF, COLS), BF16),
            vmem((4, TOK, COLS), F32),
            vmem((4, 4, TOK, COLS), BF16),
            vmem((4, 4, TOK, COLS), BF16),
            vmem((4, TOK, COLS), BF16),
            vmem((4, TOK, COLS), BF16),
            vmem((TOK, FF), BF16),
            vmem((TOK, FF), F32),
            vmem((TOK, COLS), F32),
            pltpu.SemaphoreType.DMA((8,)),
            pltpu.SemaphoreType.DMA((N_SENT,)),
            pltpu.SemaphoreType.DMA((N_RECV,)),
        ],
        compiler_params=pltpu.CompilerParams(
            collective_id=0, has_side_effects=True, vmem_limit_bytes=56 * 1024 * 1024
        ),
    )(pixels, w_embed, var_embed, var_mask, agg_query, ln_gain, w_up, w_down)


def solution(mesh):
    return jax.shard_map(
        shards,
        mesh=mesh,
        in_specs=(
            P("var", None, "seq"),
            P("var", None, None),
            P("var", None),
            P(),
            P("var"),
            P(),
            P("seq", "var"),
            P("var", "seq"),
        ),
        out_specs=P("seq", "var"),
        check_vma=False,
    )
```

```python
import math

import jax
import jax.numpy as jnp
from jax import lax
from jax.experimental import pallas as pl
from jax.experimental.pallas import tpu as pltpu
from jax.sharding import PartitionSpec as P

MESH = pl.DeviceIdType.MESH
F32, BF16 = jnp.float32, jnp.bfloat16
PIX, HS = 4, 128
N_VARS = 96
OWN_VARS = 6
ROWS = 32
DEPTH = 16 * ROWS
TOK, COLS, D, FF = 128, 256, 4096, 512
N_SENT, N_RECV = 14, 120
SPLIT = (2, 4)
SPLIT_NEAR = (2, 2)
ORDER = (
    ("x0", 0), ("z0", 0), ("pack",), ("start",), ("X", 0, 0, 1, 1), ("x0", 1), ("X", 0, 0, -1, 0), ("X", 1, 0, -1, 0),
    ("z0", 1), ("X", 1, 0, 1, 1), ("Z", 0, 1, 1), ("py",), ("Z", 0, -1, 0), ("ty",), ("z1", 1), ("ts",),
    ("XR", 0, 0, 2), ("Z", 0, -1, 1), ("agg",), ("Z", 0, 1, 0), ("X", 0, -1, 1, 1), ("z1", 2), ("XR", 0, -1, 1),
    ("X", 0, 1, 1, 1), ("S", 0, -1, 0), ("X", 0, -1, -1, 0), ("XR", 0, -1, 2), ("z1", 0), ("X", 0, 1, -1, 0),
    ("Z2", 0, 0), ("z1", 3), ("XR", 0, 0, -1), ("ayz", 1), ("XR", 0, 1, -1), ("ayz", 2), ("X", 0, 2, 1, 1),
    ("X", 0, 2, -1, 0), ("ayz", 3), ("Z", 1, 1, 2), ("Z", 1, -1, 2), ("Z", 1, -1, 1), ("XR", 0, 2, -1),
    ("XR", 0, 2, 1), ("Z", 1, 1, 1), ("XR", 0, 1, 2), ("S", 0, 1, 0), ("XR", 0, -1, -1), ("Z", 1, -1, 0),
    ("XR", 0, 0, 1), ("S", 0, 2, 0), ("Z", 1, -1, 3), ("Z", 1, 1, 3), ("XR", 1, 0, -1), ("Z", 1, 1, 0),
    ("X", 1, 1, 1, 2), ("XR", 0, 1, 1), ("XR", 0, 2, 2), ("X", 1, -1, -1, 1), ("XR", 1, 0, 2), ("ln",),
    ("X", 1, -1, 1, 2), ("up", 0), ("XR", 1, 0, 1), ("up", 1), ("up", -1), ("up", 2), ("S", 1, 1, 0),
    ("X", 1, -1, -1, 0), ("hid",), ("dp", 0, 0), ("XR", 1, -1, -1), ("X", 1, -1, 1, 3), ("S", 1, -1, 0),
    ("X", 1, 1, 1, 3), ("X", 1, 1, -1, 0), ("XR", 1, -1, 1), ("dp", 0, -1), ("XR", 1, 1, 1), ("Z2", 1, 1),
    ("dp", 1, 0), ("X", 1, 1, -1, 1), ("dp", 0, 2), ("dp", 0, 1), ("dp", -1, -1), ("dp", -1, 0), ("Z2", 1, 0),
    ("XR", 1, -1, 2), ("dp", -1, 1), ("X", 1, 2, -1, 1), ("X", 1, 2, 1, 2), ("XR", 1, 1, -1), ("dp", -1, 2),
    ("dp", 1, -1), ("XR", 1, 1, 2), ("dp", 1, 1), ("S", 1, 2, 0), ("X", 1, 2, -1, 0), ("X", 1, 2, 1, 3), ("dp", 1, 2),
    ("XR", 1, 2, 1), ("XR", 1, 2, -1), ("dp", 2, 0), ("ds", 0), ("dp", 2, 1), ("dp", 2, -1), ("XR", 1, 2, 2),
    ("ds", -1), ("dp", 2, 2), ("ds", 1), ("sent",), ("ds", 2), ("fin",),
)


def block_of(iota):
    block, row = iota // ROWS, iota % ROWS
    owner = (block % 4) * 4 + block // 4
    local = jnp.where(row < OWN_VARS * PIX, row // PIX, row - OWN_VARS * PIX)
    return owner * OWN_VARS + local, row < OWN_VARS * (PIX + 1)


def kernel(
    pix_in, emb_in, bias_in, mask_in, query_in, gain_in, up_in, down_in, out,
    pix, emb, bias, mask, query, gain, rows_f, pix_f,
    tab_out, tab_mid, tab, pat, agg, norm, up, down, own_sum, term, got_y, got_z, summed, hidden_ref, part, total,
    local_sem, send_sem, recv_sem,
):
    var, seq = lax.axis_index("var"), lax.axis_index("seq")
    zl, y = var // 4, lax.rem(var, 4)
    zh, x, core = seq // 8, lax.rem(seq // 2, 4), lax.rem(seq, 2)
    z = zh * 4 + zl
    other = 1 - core

    def mod4(v):
        return lax.rem(v + 4, 4)

    def at_var(zl_, y_):
        return (zl_ * 4 + y_, seq)

    def at_seq(a, b, core_):
        return (var, mod4(zh + a) * 8 + mod4(x + b) * 2 + core_)

    def at_z(d):
        z_ = lax.rem(z + d + 16, 16)
        return (lax.rem(z_, 4) * 4 + y, (z_ // 4) * 8 + x * 2 + core)

    sibling = at_seq(0, 0, other)

    locals_ = []
    for i, (src, dst) in enumerate(
        (
            (pix_in, pix),
            (emb_in, emb),
            (bias_in, bias),
            (mask_in, mask),
            (query_in, query),
            (gain_in, gain),
            (up_in, up.at[zh, x, core]),
            (down_in, down.at[zh, x, :, pl.ds(pl.multiple_of(core * HS, HS), HS)]),
        )
    ):
        locals_.append(pltpu.make_async_copy(src, dst, local_sem.at[i]))
        locals_[-1].start()

    barrier = pltpu.get_barrier_semaphore()
    peers = [at_z(1), at_z(-1), at_z(2), at_z(-2), sibling]
    peers += [at_var(mod4(zl + i), y) for i in (1, 2, 3)]
    peers += [at_var(zl, mod4(y + i)) for i in (1, 2, 3)]
    peers += [at_seq(1, 0, core), at_seq(-1, 0, core), at_seq(0, 1, core), at_seq(0, -1, core)]
    for peer in peers:
        pl.semaphore_signal(barrier, inc=1, device_id=peer, device_id_type=MESH)

    groups, keys = {}, {}

    def sem_of(key):
        return keys.setdefault(key, len(keys))

    def copy_of(src, dst, group, key, device):
        return pltpu.make_async_remote_copy(
            src_ref=src,
            dst_ref=dst,
            send_sem=send_sem.at[groups.setdefault(group, len(groups))],
            recv_sem=recv_sem.at[sem_of(key)],
            device_id=device,
            device_id_type=MESH,
        )

    def send(src, dst, group, key, device):
        copy_of(src, dst, group, key, device).start()

    def recv(view, key):
        copy_of(view, view, next(iter(groups)), key, sibling).wait_recv()

    def sent(view, group):
        copy_of(view, view, group, next(iter(keys)), sibling).wait_send()

    pl.semaphore_wait(barrier, len(peers))


    def pieces(m, a):
        return (SPLIT if a % 4 else SPLIT_NEAR)[m]

    def rows_of(m, a, p, count=1):
        n = (HS, FF)[m] // pieces(m, a)
        return pl.ds(p * n, n * count)

    def block(m, a, b, core_):
        if m == 0:
            return up.at[mod4(zh + a), mod4(x + b), core_]
        return down.at[mod4(zh + a), mod4(x + b), :, pl.ds(pl.multiple_of(core_ * HS, HS), HS)]

    def piece(m, a, b, p, count=1):
        if m == 0:
            return block(m, a, b, core).at[rows_of(m, a, p, count)]
        cols = pl.ds(pl.multiple_of(core * HS, HS), HS)
        return down.at[mod4(zh + a), mod4(x + b), rows_of(m, a, p, count), cols]

    def z_key(m, a, p):
        return ("z", m, a % 4, p)

    def x_key(m, a, b, p):
        n = pieces(m, a)
        alone = (b % 4 == 3 and p < n // 2) or (b % 4 == 1 and p >= n // 2)
        return ("x", m, a % 4, b % 4, p if alone else "rest")

    def z_send(m, a, p, way):
        step = {"z+": 1, "z-": -1}[way]
        if a == 0:
            rows = rows_of(m, 1, p)
            src = (up_in, down_in)[m].at[rows]
            if m == 0:
                dst = up.at[zh, x, core].at[rows]
            else:
                dst = down.at[zh, x, rows, pl.ds(pl.multiple_of(core * HS, HS), HS)]
        else:
            src = dst = piece(m, a, 0, p)
        send(src, dst, ("z", m), z_key(m, a - step, p), at_seq(step, 0, core))

    def x_send(m, a, b, p, way):
        step = {"x+": 1, "x-": -1}[way]
        src = dst = piece(m, a, b, p)
        if a == 0 and b == 0:
            src = (up_in, down_in)[m].at[rows_of(m, 0, p)]
        send(src, dst, ("x", m), x_key(m, a, b - step, p), at_seq(0, step, core))

    def s_key(m, a, b):
        return ("s", m, a % 4, b % 4 if m == 1 and a else 0)

    def swap(m, a, b):
        place = block(m, a, b, core)
        src = (up_in, down_in)[m] if a == 0 and b == 0 else place
        send(src, place, ("s", m), s_key(m, a, b), sibling)

    def z_first(m, i):
        z_send(m, 0, i, "z+")
        z_send(m, 0, pieces(m, 1) - 1 - i, "z-")

    def x_first(m):
        n = pieces(m, 0)
        for i in range(n):
            x_send(m, 0, 0, i, "x+")
            x_send(m, 0, 0, n - 1 - i, "x-")
        swap(m, 0, 0)

    def z_piece(m, a, p):
        n = pieces(m, a)
        recv(piece(m, a, 0, p), z_key(m, a, p))
        if a == -1 and p < n // 2:
            z_send(m, a, p, "z+")
        if a == 1 and p >= n // 2:
            z_send(m, a, p, "z-")
        x_send(m, a, 0, p, "x+")
        x_send(m, a, 0, p, "x-")

    def z_far(m, low):
        high = pieces(m, 2) - 1 - low
        for p in (low, high):
            recv(piece(m, 2, 0, p), z_key(m, 2, p))
        x_send(m, 2, 0, low, "x+")
        x_send(m, 2, 0, high, "x-")
        x_send(m, 2, 0, high, "x+")
        x_send(m, 2, 0, low, "x-")

    def x_piece(m, a, b, p):
        recv(piece(m, a, b, p), x_key(m, a, b, p))
        x_send(m, a, b, p, "x+" if b == -1 else "x-")

    def x_rest(m, a, b):
        n = pieces(m, a)
        first, count = {-1: (n // 2, n // 2), 1: (0, n // 2), 2: (0, n)}[b]
        recv(piece(m, a, b, first, count), x_key(m, a, b, first))
        swap(m, a, b)

    def pack():
        for i in range(3):
            locals_[i].wait()
        rows_f[:, OWN_VARS * (PIX + 1) :, :] = jnp.zeros((16, ROWS - OWN_VARS * (PIX + 1), HS), F32)
        for j in range(16):
            col = pl.ds(pl.multiple_of(j * COLS + core * HS, HS), HS)
            for v in range(OWN_VARS):
                rows_f[j, v * PIX : (v + 1) * PIX, :] = emb[v, :, col].astype(F32)
            rows_f[j, OWN_VARS * PIX : OWN_VARS * (PIX + 1), :] = bias[:, col].astype(F32)
        for j in range(16):
            tab_out[j // 4, j % 4] = rows_f[j].astype(BF16)
        row = lax.broadcasted_iota(jnp.int32, (ROWS, TOK), 0)
        pix_f[...] = jnp.where(row < OWN_VARS * (PIX + 1), 1.0, 0.0)
        for v in range(OWN_VARS):
            pix_f[v * PIX : (v + 1) * PIX, :] = pix[v].astype(F32)
        pat[y, zl] = pix_f[...].astype(BF16)
        tab_mid[zl] = tab_out[zl]

    def start():
        for i in (1, 2, 3):
            send(pat.at[y, zl], pat.at[y, zl], "pz", "pz", at_var(mod4(zl + i), y))
        for i, step in ((1, 1), (3, -1), (2, 2 - 4 * core)):
            send(tab_out.at[mod4(zl + i)], tab_mid.at[zl], "tz", "tz", at_z(step))

    def points_y():
        recv(pat.at[0, 0:3], "pz")
        for i in (1, 2, 3):
            send(pat.at[y], pat.at[y], "py", "py", at_var(zl, mod4(y + i)))

    def table_y():
        recv(tab_mid.at[0:3], "tz")
        for i in (1, 2, 3):
            y_ = mod4(y + i)
            send(tab_mid.at[:, y_], tab.at[core, y], "ty", "ty", at_var(zl, y_))
        tab[core, y] = tab_mid[:, y]

    def table_swap():
        recv(tab.at[core, 0:3], "ty")
        send(tab.at[core], tab.at[core], "ts", "ts", sibling)

    def aggregate():
        recv(pat.at[0:3], "py")
        recv(tab.at[other], "ts")
        locals_[3].wait()
        locals_[4].wait()
        points = pat[...].reshape(DEPTH, TOK)
        points_f = points.astype(F32)
        twice = jnp.concatenate([points_f, points_f], axis=1)
        query_f = query[...].astype(F32).reshape(1, COLS)
        tables = [tab[h].reshape(DEPTH, HS) for h in range(2)]
        shares = []
        for h in range(2):
            dots = jnp.sum(tables[h].astype(F32) * query_f[:, h * HS : (h + 1) * HS], axis=1, keepdims=True)
            shares.append((dots * (1.0 / math.sqrt(HS))) * points_f)
        share = jnp.concatenate(shares, axis=1)
        which, real = block_of(lax.broadcasted_iota(jnp.int32, (N_VARS, DEPTH), 1))
        collect = jnp.where(
            (which == lax.broadcasted_iota(jnp.int32, (N_VARS, DEPTH), 0)) & real, 1.0, 0.0
        ).astype(BF16)
        scores = jnp.zeros((N_VARS, COLS), F32)
        for _ in range(3):
            piece = share.astype(BF16)
            share = share - piece.astype(F32)
            scores = scores + jnp.dot(collect, piece, preferred_element_type=F32)
        diagonal = lax.broadcasted_iota(jnp.int32, (N_VARS, N_VARS), 0) == lax.broadcasted_iota(
            jnp.int32, (N_VARS, N_VARS), 1
        )
        keep = jnp.sum(
            jnp.where(diagonal, mask[...].astype(F32).reshape(1, N_VARS), 0.0), axis=1, keepdims=True
        )
        scores = jnp.where(keep > 0.0, scores, -1e30)
        expo = jnp.exp(scores - jnp.max(scores, axis=0, keepdims=True))
        weights = (expo / jnp.sum(expo, axis=0, keepdims=True)).astype(BF16)
        which, real = block_of(lax.broadcasted_iota(jnp.int32, (DEPTH, N_VARS), 0))
        expand = jnp.where(
            (which == lax.broadcasted_iota(jnp.int32, (DEPTH, N_VARS), 1)) & real, 1.0, 0.0
        ).astype(BF16)
        mixed = jnp.dot(expand, weights, preferred_element_type=F32) * twice
        high = mixed.astype(BF16)
        low = (mixed - high.astype(F32)).astype(BF16)
        over_rows = (((0,), (0,)), ((), ()))
        merged = []
        for h in range(2):
            cols = slice(h * HS, (h + 1) * HS)
            merged.append(
                lax.dot_general(high[:, cols], tables[h], over_rows, preferred_element_type=F32)
                + lax.dot_general(low[:, cols], tables[h], over_rows, preferred_element_type=F32)
            )
        agg[var] = jnp.concatenate(merged, axis=1).astype(BF16)

        for i in (1, 2, 3):
            send(agg.at[var], agg.at[var], "agg", ("az", i), at_var(mod4(zl + i), y))
        for i in (1, 3, 2):
            send(agg.at[var], agg.at[var], "agg", "ay", at_var(zl, mod4(y + i)))

    def features_y(j):
        place = agg.at[mod4(zl - j) * 4 + y]
        recv(place, ("az", j))
        for i in (1, 3, 2):
            send(place, place, "agg", "ay", at_var(zl, mod4(y + i)))

    def layer_norm():
        recv(agg.at[0:12], "ay")
        sums = jnp.zeros((TOK, COLS), F32)
        for v in range(16):
            sums = sums + agg[v].astype(F32)
        mean = jnp.sum(sums, axis=1, keepdims=True) * (1.0 / D)
        sums = jnp.zeros((TOK, COLS), F32)
        for v in range(16):
            centered = agg[v].astype(F32) - mean
            sums = sums + centered * centered
        variance = jnp.sum(sums, axis=1, keepdims=True) * (1.0 / D)
        scale = lax.rsqrt(variance + 1e-05)
        locals_[5].wait()
        for v in range(16):
            cols = slice(v * COLS, (v + 1) * COLS)
            gains = gain[cols].astype(F32).reshape(1, COLS)
            norm[v // 4, :, (v % 4) * COLS : (v % 4 + 1) * COLS] = (
                (agg[v].astype(F32) - mean) * scale * gains
            ).astype(BF16)

    def up_part(a):
        if a == 0:
            locals_[6].wait()
        q = mod4(zh + a)
        recv(up.at[q, :, other], s_key(0, a, 0))
        value = jnp.dot(norm[q], up[q].reshape(1024, FF), preferred_element_type=F32)
        part[...] = value if a == 0 else part[...] + value

    def activate():
        hidden_ref[...] = jax.nn.gelu(part[...], approximate=True).astype(BF16)

    def down_part(a, b):
        if a == 0 and b == 0:
            locals_[7].wait()
        q, y_ = mod4(zh + a), mod4(x + b)
        cols = pl.ds(pl.multiple_of(other * HS, HS), HS)
        if a:
            recv(down.at[q, y_, :, cols], s_key(1, a, b))
        elif b == 0:
            recv(down.at[q, :, :, cols], s_key(1, a, b))
        value = jnp.dot(hidden_ref[...], down[q, y_], preferred_element_type=F32)
        away = mod4(y_ - y)

        @pl.when(away == 0)
        def _():
            own_sum[a % 4] = value

        term[a % 4, b % 4] = value.astype(BF16)

        @pl.when(away != 0)
        def _():
            send(term.at[a % 4, b % 4], got_y.at[a % 4, away], "ry", ("ry", a % 4), at_var(zl, y_))

    def down_sum(a):
        a = a % 4
        q = mod4(zh + a)
        recv(got_y.at[a, 1:4], ("ry", a))
        value = own_sum[a]
        for i in (1, 2, 3):
            value = value + got_y[a, i].astype(F32)
        away = mod4(zl - q)

        @pl.when(away == 0)
        def _():
            total[...] = value

        summed[a] = value.astype(BF16)

        @pl.when(away != 0)
        def _():
            send(summed.at[a], got_z.at[away], "rz", "rz", at_var(q, y))

    def all_sent():
        for m in (0, 1):
            sent(up.at[0, 0:3, 0], ("z", m))
            sent(up.at[0:3, :, 0], ("x", m))
            sent(up.at[0:2], ("s", m))
        sent(pat.at[0, 0:3], "pz")
        sent(pat.at[0:3], "py")
        sent(tab_mid.at[0:3], "tz")
        sent(tab_mid.at[0:3], "ty")
        sent(tab.at[0], "ts")
        sent(agg.at[0:15], "agg")

    def finish():
        result = agg[var].astype(F32) + total[...]
        recv(got_z.at[1:4], "rz")
        for i in (1, 2, 3):
            result = result + got_z[i].astype(F32)
        out[...] = result.astype(BF16)
        sent(got_y.at[0:3], "ry")
        sent(got_z.at[0:3], "rz")

    steps = {
        "pack": pack,
        "start": start,
        "z0": lambda i: z_first(0, i),
        "x0": x_first,
        "z1": lambda i: z_first(1, i),
        "Z": z_piece,
        "Z2": z_far,
        "X": x_piece,
        "XR": x_rest,
        "S": swap,
        "py": points_y,
        "ty": table_y,
        "ts": table_swap,
        "agg": aggregate,
        "ayz": features_y,
        "ln": layer_norm,
        "up": up_part,
        "hid": activate,
        "dp": down_part,
        "sent": all_sent,
        "ds": down_sum,
        "fin": finish,
    }
    for name, *rest in ORDER:
        steps[name](*rest)
    assert len(keys) <= N_RECV and len(groups) <= N_SENT


def shards(pixels, w_embed, var_embed, var_mask, agg_query, ln_gain, w_up, w_down):
    vmem = pltpu.VMEM
    return pl.pallas_call(
        kernel,
        out_shape=jax.ShapeDtypeStruct((TOK, COLS), BF16),
        in_specs=[pl.BlockSpec(memory_space=pl.ANY)] * 8,
        out_specs=pl.BlockSpec(memory_space=pltpu.VMEM),
        scratch_shapes=[
            vmem((OWN_VARS, PIX, TOK), BF16),
            vmem((OWN_VARS, PIX, D), BF16),
            vmem((OWN_VARS, D), BF16),
            vmem((N_VARS,), jnp.int32),
            vmem((COLS,), BF16),
            vmem((D,), BF16),
            vmem((16, ROWS, HS), F32),
            vmem((ROWS, TOK), F32),
            vmem((4, 4, ROWS, HS), BF16),
            vmem((4, 4, ROWS, HS), BF16),
            vmem((2, 4, 4, ROWS, HS), BF16),
            vmem((4, 4, ROWS, TOK), BF16),
            vmem((16, TOK, COLS), BF16),
            vmem((4, TOK, 1024), BF16),
            vmem((4, 4, 2, 128, FF), BF16),
            vmem((4, 4, FF, COLS), BF16),
            vmem((4, TOK, COLS), F32),
            vmem((4, 4, TOK, COLS), BF16),
            vmem((4, 4, TOK, COLS), BF16),
            vmem((4, TOK, COLS), BF16),
            vmem((4, TOK, COLS), BF16),
            vmem((TOK, FF), BF16),
            vmem((TOK, FF), F32),
            vmem((TOK, COLS), F32),
            pltpu.SemaphoreType.DMA((8,)),
            pltpu.SemaphoreType.DMA((N_SENT,)),
            pltpu.SemaphoreType.DMA((N_RECV,)),
        ],
        compiler_params=pltpu.CompilerParams(
            collective_id=0, has_side_effects=True, vmem_limit_bytes=56 * 1024 * 1024
        ),
    )(pixels, w_embed, var_embed, var_mask, agg_query, ln_gain, w_up, w_down)


def solution(mesh):
    return jax.shard_map(
        shards,
        mesh=mesh,
        in_specs=(
            P("var", None, "seq"),
            P("var", None, None),
            P("var", None),
            P(),
            P("var"),
            P(),
            P("seq", "var"),
            P("var", "seq"),
        ),
        out_specs=P("seq", "var"),
        check_vma=False,
    )
```

```python
import math

import jax
import jax.numpy as jnp
from jax import lax
from jax.experimental import pallas as pl
from jax.experimental.pallas import tpu as pltpu
from jax.sharding import PartitionSpec as P

MESH = pl.DeviceIdType.MESH
F32, BF16 = jnp.float32, jnp.bfloat16
PIX, HS = 4, 128
N_VARS = 96
OWN_VARS = 6
ROWS = 32
DEPTH = 16 * ROWS
TOK, COLS, D, FF = 128, 256, 4096, 512
N_SENT, N_RECV = 15, 120
SPLIT = (2, 4)
SPLIT_NEAR = (2, 2)
ORDER = (
    ("pack",), ("start",), ("z0", 0), ("z0", 1), ("x0", 0), ("x0", 1), ("X", 0, 0, -1, 0), ("X", 0, 0, 1, 1),
    ("XR", 0, 0, -1), ("XR", 0, 0, 1), ("py",), ("X", 1, 0, -1, 0), ("X", 1, 0, 1, 1), ("tz",), ("XR", 1, 0, -1),
    ("XR", 1, 0, 1), ("XR", 0, 0, 2), ("XR", 1, 0, 2), ("Z", 0, -1, 0), ("Z", 0, 1, 1), ("z1", 0), ("z1", 1),
    ("z1", 2), ("z1", 3), ("tx",), ("X", 0, -1, -1, 0), ("agg", 0), ("Z", 0, -1, 1), ("S", 0, -1, 0), ("Z", 0, 1, 0),
    ("S", 0, 1, 0), ("X", 0, 1, 1, 1), ("tsib", -1), ("tsib", 1), ("Z2", 0, 0), ("S", 0, 2, 0), ("agg", -1),
    ("agg", 1), ("Z", 1, -1, 0), ("X", 0, -1, 1, 1), ("XR", 0, -1, 1), ("Z", 1, 1, 3), ("tsib", 2), ("XR", 0, -1, -1),
    ("XR", 0, 1, 1), ("agg", 2), ("X", 0, 1, -1, 0), ("XR", 0, 1, -1), ("Z", 1, -1, 1), ("Z", 1, 1, 2),
    ("X", 0, 2, -1, 0), ("X", 0, 2, 1, 1), ("Z", 1, -1, 2), ("Z", 1, 1, 1), ("XR", 0, 2, -1), ("XR", 0, 2, 1),
    ("X", 1, -1, -1, 0), ("XR", 0, -1, 2), ("Z", 1, -1, 3), ("S", 1, -1, 0), ("Z", 1, 1, 0), ("XR", 0, 1, 2),
    ("S", 1, 1, 0), ("X", 1, 1, 1, 3), ("X", 1, -1, -1, 1), ("ln",), ("Z2", 1, 0), ("XR", 0, 2, 2), ("X", 1, 1, 1, 2),
    ("up", 0), ("X", 1, -1, 1, 2), ("up", -1), ("X", 1, 1, -1, 1), ("up", 1), ("X", 1, -1, 1, 3), ("XR", 1, -1, 1),
    ("Z2", 1, 1), ("S", 1, 2, 0), ("XR", 1, -1, -1), ("XR", 1, 1, 1), ("up", 2), ("X", 1, 1, -1, 0), ("XR", 1, 1, -1),
    ("hid",), ("dp", 0, 0), ("X", 1, 2, 1, 3), ("dp", 0, -1), ("dp", 0, 1), ("X", 1, 2, -1, 0), ("dp", 0, 2),
    ("dp", -1, 0), ("dp", -1, -1), ("dp", -1, 1), ("dp", 1, 0), ("dp", 1, -1), ("dp", 1, 1), ("dp", 2, 0),
    ("X", 1, 2, -1, 1), ("XR", 1, -1, 2), ("XR", 1, 2, -1), ("X", 1, 2, 1, 2), ("dp", -1, 2), ("XR", 1, 1, 2),
    ("XR", 1, 2, 1), ("dp", 2, -1), ("dp", 1, 2), ("dp", 2, 1), ("XR", 1, 2, 2), ("ds", 0), ("dp", 2, 2), ("ds", -1),
    ("ds", 1), ("ds", 2, 0), ("sent",), ("ds", 2, 1), ("fin",),
)


def block_of(iota):
    owner, row = iota // ROWS, iota % ROWS
    local = jnp.where(row < OWN_VARS * PIX, row // PIX, row - OWN_VARS * PIX)
    return owner * OWN_VARS + local, row < OWN_VARS * (PIX + 1)


def kernel(
    pix_in, emb_in, bias_in, mask_in, query_in, gain_in, up_in, down_in, out,
    pix, emb, bias, mask, query, gain, rows_f, pix_f,
    tab_out, tab_mid, tab, collect, expand, pat, agg, norm, up, down, own_sum, term, got_y, got_z, summed, hidden_ref, part, total,
    local_sem, send_sem, recv_sem,
):
    var, seq = lax.axis_index("var"), lax.axis_index("seq")
    zl, y = var // 4, lax.rem(var, 4)
    zh, x, core = seq // 8, lax.rem(seq // 2, 4), lax.rem(seq, 2)
    z = zh * 4 + zl
    other = 1 - core

    def mod4(v):
        return lax.rem(v + 4, 4)

    def at_var(zl_, y_):
        return (zl_ * 4 + y_, seq)

    def at_seq(a, b, core_):
        return (var, mod4(zh + a) * 8 + mod4(x + b) * 2 + core_)

    def at_z(d):
        z_ = lax.rem(z + d + 16, 16)
        return (lax.rem(z_, 4) * 4 + y, (z_ // 4) * 8 + x * 2 + core)

    sibling = at_seq(0, 0, other)

    locals_ = []
    for i, (src, dst) in enumerate(
        (
            (pix_in, pix),
            (emb_in, emb),
            (bias_in, bias),
            (mask_in, mask),
            (query_in, query),
            (gain_in, gain),
            (up_in, up.at[zh, x, core]),
            (down_in, down.at[zh, x, :, pl.ds(pl.multiple_of(core * HS, HS), HS)]),
        )
    ):
        locals_.append(pltpu.make_async_copy(src, dst, local_sem.at[i]))
        locals_[-1].start()

    barrier = pltpu.get_barrier_semaphore()
    peers = [at_z(1), at_z(-1), at_z(2), at_z(-2), sibling]
    peers += [at_var(mod4(zl + i), y) for i in (1, 2, 3)]
    peers += [at_var(zl, mod4(y + i)) for i in (1, 2, 3)]
    peers += [at_seq(1, 0, core), at_seq(-1, 0, core)]
    peers += [at_seq(0, i, core) for i in (1, 2, 3)]
    for peer in peers:
        pl.semaphore_signal(barrier, inc=1, device_id=peer, device_id_type=MESH)

    groups, keys = {}, {}

    def sem_of(key):
        return keys.setdefault(key, len(keys))

    def copy_of(src, dst, group, key, device):
        return pltpu.make_async_remote_copy(
            src_ref=src,
            dst_ref=dst,
            send_sem=send_sem.at[groups.setdefault(group, len(groups))],
            recv_sem=recv_sem.at[sem_of(key)],
            device_id=device,
            device_id_type=MESH,
        )

    def send(src, dst, group, key, device):
        copy_of(src, dst, group, key, device).start()

    def recv(view, key):
        copy_of(view, view, next(iter(groups)), key, sibling).wait_recv()

    def sent(view, group):
        copy_of(view, view, group, next(iter(keys)), sibling).wait_send()

    pl.semaphore_wait(barrier, len(peers))


    def pieces(m, a):
        return (SPLIT if a % 4 else SPLIT_NEAR)[m]

    def rows_of(m, a, p, count=1):
        n = (HS, FF)[m] // pieces(m, a)
        return pl.ds(p * n, n * count)

    def block(m, a, b, core_):
        if m == 0:
            return up.at[mod4(zh + a), mod4(x + b), core_]
        return down.at[mod4(zh + a), mod4(x + b), :, pl.ds(pl.multiple_of(core_ * HS, HS), HS)]

    def piece(m, a, b, p, count=1):
        if m == 0:
            return block(m, a, b, core).at[rows_of(m, a, p, count)]
        cols = pl.ds(pl.multiple_of(core * HS, HS), HS)
        return down.at[mod4(zh + a), mod4(x + b), rows_of(m, a, p, count), cols]

    def z_key(m, a, p):
        return ("z", m, a % 4, p)

    def x_key(m, a, b, p):
        n = pieces(m, a)
        alone = (b % 4 == 3 and p < n // 2) or (b % 4 == 1 and p >= n // 2)
        return ("x", m, a % 4, b % 4, p if alone else "rest")

    def z_send(m, a, p, way):
        step = {"z+": 1, "z-": -1}[way]
        if a == 0:
            rows = rows_of(m, 1, p)
            src = (up_in, down_in)[m].at[rows]
            if m == 0:
                dst = up.at[zh, x, core].at[rows]
            else:
                dst = down.at[zh, x, rows, pl.ds(pl.multiple_of(core * HS, HS), HS)]
        else:
            src = dst = piece(m, a, 0, p)
        send(src, dst, ("z", m), z_key(m, a - step, p), at_seq(step, 0, core))

    def x_send(m, a, b, p, way):
        step = {"x+": 1, "x-": -1}[way]
        src = dst = piece(m, a, b, p)
        if a == 0 and b == 0:
            src = (up_in, down_in)[m].at[rows_of(m, 0, p)]
        send(src, dst, ("x", m), x_key(m, a, b - step, p), at_seq(0, step, core))

    def s_key(m, a, b):
        return ("s", m, a % 4, b % 4 if m == 1 and a else 0)

    def swap(m, a, b):
        place = block(m, a, b, core)
        src = (up_in, down_in)[m] if a == 0 and b == 0 else place
        send(src, place, ("s", m), s_key(m, a, b), sibling)

    def z_first(m, i):
        z_send(m, 0, i, "z+")
        z_send(m, 0, pieces(m, 1) - 1 - i, "z-")

    def x_first(m):
        n = pieces(m, 0)
        for i in range(n):
            x_send(m, 0, 0, i, "x+")
            x_send(m, 0, 0, n - 1 - i, "x-")
        swap(m, 0, 0)

    def z_piece(m, a, p):
        n = pieces(m, a)
        recv(piece(m, a, 0, p), z_key(m, a, p))
        if a == -1 and p < n // 2:
            z_send(m, a, p, "z+")
        if a == 1 and p >= n // 2:
            z_send(m, a, p, "z-")
        x_send(m, a, 0, p, "x+")
        x_send(m, a, 0, p, "x-")

    def z_far(m, low):
        high = pieces(m, 2) - 1 - low
        for p in (low, high):
            recv(piece(m, 2, 0, p), z_key(m, 2, p))
        x_send(m, 2, 0, low, "x+")
        x_send(m, 2, 0, high, "x-")
        x_send(m, 2, 0, high, "x+")
        x_send(m, 2, 0, low, "x-")

    def x_piece(m, a, b, p):
        recv(piece(m, a, b, p), x_key(m, a, b, p))
        x_send(m, a, b, p, "x+" if b == -1 else "x-")

    def x_rest(m, a, b):
        n = pieces(m, a)
        first, count = {-1: (n // 2, n // 2), 1: (0, n // 2), 2: (0, n)}[b]
        recv(piece(m, a, b, first, count), x_key(m, a, b, first))
        swap(m, a, b)

    def pack():
        for i in (0, 1, 2, 4):
            locals_[i].wait()
        rows_f[:, OWN_VARS * (PIX + 1) :, :] = jnp.zeros((16, ROWS - OWN_VARS * (PIX + 1), HS), F32)
        for j in range(16):
            col = pl.ds(pl.multiple_of(j * COLS + core * HS, HS), HS)
            for v in range(OWN_VARS):
                rows_f[j, v * PIX : (v + 1) * PIX, :] = emb[v, :, col].astype(F32)
            rows_f[j, OWN_VARS * PIX : OWN_VARS * (PIX + 1), :] = bias[:, col].astype(F32)
        for j in range(16):
            tab_out[j % 4, j // 4] = rows_f[j].astype(BF16)
        row = lax.broadcasted_iota(jnp.int32, (ROWS, TOK), 0)
        pix_f[...] = jnp.where(row < OWN_VARS * (PIX + 1), 1.0, 0.0)
        for v in range(OWN_VARS):
            pix_f[v * PIX : (v + 1) * PIX, :] = pix[v].astype(F32)
        for h in range(2):
            pix_f[ROWS - 2 + h : ROWS - 1 + h, :] = query[h * HS : (h + 1) * HS].astype(F32).reshape(1, HS)
        pat[zl, y] = pix_f[...].astype(BF16)
        tab_mid[y] = tab_out[y]

    def start():
        for i in (1, 2, 3):
            send(pat.at[zl, y], pat.at[zl, y], "pz", "pz", at_var(mod4(zl + i), y))
        for i in (1, 3, 2):
            y_ = mod4(y + i)
            send(tab_out.at[y_], tab_mid.at[y], "ty", "ty", at_var(zl, y_))

    def points_y():
        recv(pat.at[0:3, 0], "pz")
        for i in (1, 3, 2):
            send(pat.at[:, y], pat.at[:, y], "py", "py", at_var(zl, mod4(y + i)))

    def table_z():
        recv(tab_mid.at[0:3], "ty")
        for step in (1, -1, 2 - 4 * core):
            send(tab_mid.at[:, x], tab.at[core, x, zl], "tz", "tz", at_z(step))
        tab[core, x, zl] = tab_mid[:, x]

    def table_x():
        recv(tab.at[core, x, 0:3], "tz")
        for b in (1, -1, 2):
            send(tab.at[core, x], tab.at[core, x], "tx", ("tx", -b % 4), at_seq(0, b, core))
        send(tab.at[core, x], tab.at[core, x], "ts", ("ts", 0), sibling)

    def table_swap(b):
        place = tab.at[core, mod4(x + b)]
        recv(place, ("tx", b % 4))
        send(place, place, "ts", ("ts", b % 4), sibling)

    def aggregate(b):
        quarter = mod4(x + b)
        if b == 0:
            recv(pat.at[0:3], "py")
            locals_[3].wait()
            for ref, dim in ((collect, 1), (expand, 0)):
                which, real = block_of(lax.broadcasted_iota(jnp.int32, ref.shape, dim))
                own = (which == lax.broadcasted_iota(jnp.int32, ref.shape, 1 - dim)) & real
                ref[...] = jnp.where(own, 1.0, 0.0).astype(BF16)
        recv(tab.at[other, quarter], ("ts", b % 4))
        points_f = pat[...].reshape(DEPTH, TOK).astype(F32)
        twice = jnp.concatenate([points_f, points_f], axis=1)
        tables = [tab[h, quarter].reshape(DEPTH, HS) for h in range(2)]
        queries = pat[quarter, y].astype(F32)
        shares = []
        for h in range(2):
            query_f = queries[ROWS - 2 + h : ROWS - 1 + h, :]
            dots = jnp.sum(tables[h].astype(F32) * query_f, axis=1, keepdims=True)
            shares.append((dots * (1.0 / math.sqrt(HS))) * points_f)
        share = jnp.concatenate(shares, axis=1)
        scores = jnp.zeros((N_VARS, COLS), F32)
        for _ in range(3):
            piece = share.astype(BF16)
            share = share - piece.astype(F32)
            scores = scores + jnp.dot(collect[...], piece, preferred_element_type=F32)
        diagonal = lax.broadcasted_iota(jnp.int32, (N_VARS, N_VARS), 0) == lax.broadcasted_iota(
            jnp.int32, (N_VARS, N_VARS), 1
        )
        keep = jnp.sum(
            jnp.where(diagonal, mask[...].astype(F32).reshape(1, N_VARS), 0.0), axis=1, keepdims=True
        )
        scores = jnp.where(keep > 0.0, scores, -1e30)
        expo = jnp.exp(scores - jnp.max(scores, axis=0, keepdims=True))
        weights = (expo / jnp.sum(expo, axis=0, keepdims=True)).astype(BF16)
        mixed = jnp.dot(expand[...], weights, preferred_element_type=F32) * twice
        high = mixed.astype(BF16)
        low = (mixed - high.astype(F32)).astype(BF16)
        over_rows = (((0,), (0,)), ((), ()))
        merged = []
        for h in range(2):
            cols = slice(h * HS, (h + 1) * HS)
            merged.append(
                lax.dot_general(high[:, cols], tables[h], over_rows, preferred_element_type=F32)
                + lax.dot_general(low[:, cols], tables[h], over_rows, preferred_element_type=F32)
            )
        place = agg.at[quarter * 4 + y]
        place[...] = jnp.concatenate(merged, axis=1).astype(BF16)
        for i in (1, 3, 2):
            send(place, place, "agg", "ay", at_var(zl, mod4(y + i)))

    def layer_norm():
        recv(agg.at[0:12], "ay")
        sums = jnp.zeros((TOK, COLS), F32)
        for v in range(16):
            sums = sums + agg[v].astype(F32)
        mean = jnp.sum(sums, axis=1, keepdims=True) * (1.0 / D)
        sums = jnp.zeros((TOK, COLS), F32)
        for v in range(16):
            centered = agg[v].astype(F32) - mean
            sums = sums + centered * centered
        variance = jnp.sum(sums, axis=1, keepdims=True) * (1.0 / D)
        scale = lax.rsqrt(variance + 1e-05)
        locals_[5].wait()
        for v in range(16):
            cols = slice(v * COLS, (v + 1) * COLS)
            gains = gain[cols].astype(F32).reshape(1, COLS)
            norm[v // 4, :, (v % 4) * COLS : (v % 4 + 1) * COLS] = (
                (agg[v].astype(F32) - mean) * scale * gains
            ).astype(BF16)

    def up_part(a):
        if a == 0:
            locals_[6].wait()
        q = mod4(zh + a)
        recv(up.at[q, :, other], s_key(0, a, 0))
        value = jnp.dot(norm[q], up[q].reshape(1024, FF), preferred_element_type=F32)
        part[...] = value if a == 0 else part[...] + value

    def activate():
        hidden_ref[...] = jax.nn.gelu(part[...], approximate=True).astype(BF16)

    def halves(a):
        n = 2 if a == 2 else 1
        return [slice(i * TOK // n, (i + 1) * TOK // n) for i in range(n)]

    def down_part(a, b):
        if a == 0 and b == 0:
            locals_[7].wait()
        q, y_ = mod4(zh + a), mod4(x + b)
        cols = pl.ds(pl.multiple_of(other * HS, HS), HS)
        if a:
            recv(down.at[q, y_, :, cols], s_key(1, a, b))
        elif b == 0:
            recv(down.at[q, :, :, cols], s_key(1, a, b))
        value = jnp.dot(hidden_ref[...], down[q, y_], preferred_element_type=F32)
        away = mod4(y_ - y)

        @pl.when(away == 0)
        def _():
            own_sum[a % 4] = value

        term[a % 4, b % 4] = value.astype(BF16)

        @pl.when(away != 0)
        def _():
            for half in halves(a):
                src, dst = term.at[a % 4, b % 4, half], got_y.at[a % 4, away, half]
                send(src, dst, "ry", ("ry", a % 4, half.start), at_var(zl, y_))

    def down_sum(a, number=0):
        a, half = a % 4, halves(a)[number]
        q = mod4(zh + a)
        recv(got_y.at[a, 1:4, half], ("ry", a, half.start))
        value = own_sum[a, half]
        for i in (1, 2, 3):
            value = value + got_y[a, i, half].astype(F32)
        away = mod4(zl - q)

        @pl.when(away == 0)
        def _():
            total[half] = value

        summed[a, half] = value.astype(BF16)

        @pl.when(away != 0)
        def _():
            send(summed.at[a, half], got_z.at[away, half], "rz", "rz", at_var(q, y))

    def all_sent():
        for m in (0, 1):
            sent(up.at[0, 0:3, 0], ("z", m))
            sent(up.at[0:3, :, 0], ("x", m))
            sent(up.at[0:2], ("s", m))
        sent(pat.at[0, 0:3], "pz")
        sent(pat.at[0:3], "py")
        sent(tab_mid.at[0:3], "tz")
        sent(tab_mid.at[0:3], "ty")
        sent(tab.at[0, 0:3], "tx")
        sent(tab.at[0], "ts")
        sent(agg.at[0:12], "agg")

    def finish():
        result = agg[var].astype(F32) + total[...]
        recv(got_z.at[1:4], "rz")
        for i in (1, 2, 3):
            result = result + got_z[i].astype(F32)
        out[...] = result.astype(BF16)
        sent(got_y.at[0:3], "ry")
        sent(got_z.at[0:3], "rz")

    steps = {
        "pack": pack,
        "start": start,
        "z0": lambda i: z_first(0, i),
        "x0": x_first,
        "z1": lambda i: z_first(1, i),
        "Z": z_piece,
        "Z2": z_far,
        "X": x_piece,
        "XR": x_rest,
        "S": swap,
        "py": points_y,
        "tz": table_z,
        "tx": table_x,
        "tsib": table_swap,
        "agg": aggregate,
        "ln": layer_norm,
        "up": up_part,
        "hid": activate,
        "dp": down_part,
        "sent": all_sent,
        "ds": down_sum,
        "fin": finish,
    }
    for name, *rest in ORDER:
        steps[name](*rest)
    assert len(keys) <= N_RECV and len(groups) <= N_SENT


def shards(pixels, w_embed, var_embed, var_mask, agg_query, ln_gain, w_up, w_down):
    vmem = pltpu.VMEM
    return pl.pallas_call(
        kernel,
        out_shape=jax.ShapeDtypeStruct((TOK, COLS), BF16),
        in_specs=[pl.BlockSpec(memory_space=pl.ANY)] * 8,
        out_specs=pl.BlockSpec(memory_space=pltpu.VMEM),
        scratch_shapes=[
            vmem((OWN_VARS, PIX, TOK), BF16),
            vmem((OWN_VARS, PIX, D), BF16),
            vmem((OWN_VARS, D), BF16),
            vmem((N_VARS,), jnp.int32),
            vmem((COLS,), BF16),
            vmem((D,), BF16),
            vmem((16, ROWS, HS), F32),
            vmem((ROWS, TOK), F32),
            vmem((4, 4, ROWS, HS), BF16),
            vmem((4, 4, ROWS, HS), BF16),
            vmem((2, 4, 4, 4, ROWS, HS), BF16),
            vmem((N_VARS, DEPTH), BF16),
            vmem((DEPTH, N_VARS), BF16),
            vmem((4, 4, ROWS, TOK), BF16),
            vmem((16, TOK, COLS), BF16),
            vmem((4, TOK, 1024), BF16),
            vmem((4, 4, 2, 128, FF), BF16),
            vmem((4, 4, FF, COLS), BF16),
            vmem((4, TOK, COLS), F32),
            vmem((4, 4, TOK, COLS), BF16),
            vmem((4, 4, TOK, COLS), BF16),
            vmem((4, TOK, COLS), BF16),
            vmem((4, TOK, COLS), BF16),
            vmem((TOK, FF), BF16),
            vmem((TOK, FF), F32),
            vmem((TOK, COLS), F32),
            pltpu.SemaphoreType.DMA((8,)),
            pltpu.SemaphoreType.DMA((N_SENT,)),
            pltpu.SemaphoreType.DMA((N_RECV,)),
        ],
        compiler_params=pltpu.CompilerParams(
            collective_id=0, has_side_effects=True, vmem_limit_bytes=56 * 1024 * 1024
        ),
    )(pixels, w_embed, var_embed, var_mask, agg_query, ln_gain, w_up, w_down)


def solution(mesh):
    return jax.shard_map(
        shards,
        mesh=mesh,
        in_specs=(
            P("var", None, "seq"),
            P("var", None, None),
            P("var", None),
            P(),
            P("var"),
            P(),
            P("seq", "var"),
            P("var", "seq"),
        ),
        out_specs=P("seq", "var"),
        check_vma=False,
    )
```

```python
import math

import jax
import jax.numpy as jnp
from jax import lax
from jax.experimental import pallas as pl
from jax.experimental.pallas import tpu as pltpu
from jax.sharding import PartitionSpec as P

MESH = pl.DeviceIdType.MESH
F32, BF16 = jnp.float32, jnp.bfloat16
PIX, HS = 4, 128
N_VARS = 96
OWN_VARS = 6
ROWS = 32
DEPTH = 16 * ROWS
TOK, COLS, D, FF = 128, 256, 4096, 512
N_SENT, N_RECV = 15, 120
SPLIT = (4, 4)
SPLIT_NEAR = (2, 2)
ORDER = (
    ("x0", 0), ("z0", 0), ("pack",), ("z0", 1), ("start",), ("x0", 1), ("tz",), ("z0", 2), ("X", 0, 0, 1, 1),
    ("X", 1, 0, -1, 0), ("Z", 0, 1, 3), ("py",), ("z0", 3), ("Z", 0, -1, 0), ("X", 1, 0, 1, 1), ("tx",),
    ("X", 0, 0, -1, 0), ("X", 0, 1, 1, 3), ("XR", 0, 0, 1), ("Z", 0, -1, 1), ("Z", 0, 1, 2), ("agg", 0), ("z1", 0),
    ("Z", 0, 1, 1), ("tsib", 1), ("tsib", -1), ("Z", 0, -1, 3), ("X", 0, -1, -1, 0), ("agg", -1), ("Z", 0, -1, 2),
    ("XR", 0, 0, -1), ("X", 0, -1, -1, 1), ("z1", 1), ("Z", 0, 1, 0), ("z1", 2), ("X", 0, 1, -1, 1), ("agg", 1),
    ("X", 0, 1, 1, 2), ("tsib", 2), ("XR", 1, 0, 1), ("Z2", 0, 1), ("z1", 3), ("Z2", 0, 0), ("agg", 2),
    ("XR", 0, 0, 2), ("X", 0, -1, 1, 3), ("Z", 1, 1, 3), ("X", 0, 1, -1, 0), ("S", -1, 0), ("X", 0, -1, 1, 2),
    ("X", 0, 2, -1, 0), ("X", 0, 2, 1, 3), ("X", 0, 2, -1, 1), ("S", 1, 0), ("X", 0, 2, 1, 2), ("Z", 1, 1, 1),
    ("XR", 0, 1, -1), ("Z", 1, -1, 0), ("ln",), ("Z", 1, -1, 1), ("XR", 1, 0, 2), ("XR", 0, 2, 1), ("S", 2, 0),
    ("XR", 0, 1, 2), ("XR", 0, -1, -1), ("XR", 0, -1, 1), ("Z", 1, 1, 2), ("XR", 0, 2, 2), ("Z", 1, -1, 2),
    ("XR", 0, 1, 1), ("XR", 0, 2, -1), ("Z", 1, -1, 3), ("up", 0), ("XR", 1, 0, -1), ("Z", 1, 1, 0), ("XR", 0, -1, 2),
    ("X", 1, -1, -1, 0), ("up", 1), ("up", 2), ("up", -1), ("hid",), ("X", 1, -1, -1, 1), ("X", 1, 1, 1, 3),
    ("Z2", 1, 0), ("dp", 0, 0), ("X", 1, 1, -1, 1), ("X", 1, -1, 1, 2), ("dp", -1, 0), ("X", 1, -1, 1, 3),
    ("dp", 0, 2), ("dp", 0, 1), ("dp", 1, 0), ("Z2", 1, 1), ("X", 1, 1, -1, 0), ("X", 1, 1, 1, 2), ("dp", 2, 0),
    ("XR", 1, -1, -1), ("XR", 1, -1, 1), ("X", 1, 2, 1, 3), ("dp", 0, -1), ("X", 1, 2, -1, 0), ("XR", 1, 1, -1),
    ("XR", 1, 1, 1), ("dp", -1, 1), ("dp", -1, -1), ("XR", 1, -1, 2), ("dp", -1, 2), ("dp", 1, 1), ("X", 1, 2, -1, 1),
    ("X", 1, 2, 1, 2), ("dp", 1, -1), ("XR", 1, 2, -1), ("XR", 1, 1, 2), ("dp", 1, 2), ("dp", 2, -1), ("XR", 1, 2, 1),
    ("XR", 1, 2, 2), ("ds", 0), ("dp", 2, 2), ("dp", 2, 1), ("ds", -1), ("ds", 1), ("ds", 2, 0), ("sent",),
    ("ds", 2, 1), ("fin",),
)


def block_of(iota):
    owner, row = iota // ROWS, iota % ROWS
    local = jnp.where(row < OWN_VARS * PIX, row // PIX, row - OWN_VARS * PIX)
    return owner * OWN_VARS + local, row < OWN_VARS * (PIX + 1)


def kernel(
    pix_in, emb_in, bias_in, mask_in, query_in, gain_in, up_in, down_in, out,
    pix, emb, bias, mask, query, gain, rows_f, pix_f,
    tab_out, tab_mid, tab, collect, expand, pat, agg, norm, up, down, own_sum, term, got_y, got_z, summed, hidden, part, total,
    local_sem, send_sem, recv_sem,
):
    var, seq = lax.axis_index("var"), lax.axis_index("seq")
    zl, y = var // 4, lax.rem(var, 4)
    zh, x, core = seq // 8, lax.rem(seq // 2, 4), lax.rem(seq, 2)
    z = zh * 4 + zl
    other = 1 - core

    def mod4(v):
        return lax.rem(v + 4, 4)

    def at_var(zl_, y_):
        return (zl_ * 4 + y_, seq)

    def at_seq(a, b, core_):
        return (var, mod4(zh + a) * 8 + mod4(x + b) * 2 + core_)

    def at_z(d):
        z_ = lax.rem(z + d + 16, 16)
        return (lax.rem(z_, 4) * 4 + y, (z_ // 4) * 8 + x * 2 + core)

    sibling = at_seq(0, 0, other)

    locals_ = []
    for i, (src, dst) in enumerate(
        (
            (pix_in, pix),
            (emb_in, emb),
            (bias_in, bias),
            (mask_in, mask),
            (query_in, query),
            (gain_in, gain),
            (up_in, up.at[zh, x, core]),
            (down_in, down.at[zh, x]),
        )
    ):
        locals_.append(pltpu.make_async_copy(src, dst, local_sem.at[i]))
        locals_[-1].start()

    barrier = pltpu.get_barrier_semaphore()
    peers = [at_z(1), at_z(-1), at_z(2), at_z(-2), sibling]
    peers += [at_var(mod4(zl + i), y) for i in (1, 2, 3)]
    peers += [at_var(zl, mod4(y + i)) for i in (1, 2, 3)]
    peers += [at_seq(1, 0, core), at_seq(-1, 0, core)]
    peers += [at_seq(0, i, core) for i in (1, 3)]
    for peer in peers:
        pl.semaphore_signal(barrier, inc=1, device_id=peer, device_id_type=MESH)

    groups, keys = {}, {}

    def sem_of(key):
        return keys.setdefault(key, len(keys))

    def copy_of(src, dst, group, key, device):
        return pltpu.make_async_remote_copy(
            src_ref=src,
            dst_ref=dst,
            send_sem=send_sem.at[groups.setdefault(group, len(groups))],
            recv_sem=recv_sem.at[sem_of(key)],
            device_id=device,
            device_id_type=MESH,
        )

    def send(src, dst, group, key, device):
        copy_of(src, dst, group, key, device).start()

    def recv(view, key):
        copy_of(view, view, next(iter(groups)), key, sibling).wait_recv()

    def sent(view, group):
        copy_of(view, view, group, next(iter(keys)), sibling).wait_send()

    pl.semaphore_wait(barrier, len(peers))


    def pieces(m, a):
        return (SPLIT if a % 4 else SPLIT_NEAR)[m]

    def rows_of(m, a, p, count=1):
        n = (HS, FF)[m] // pieces(m, a)
        return pl.ds(p * n, n * count)

    def block(m, a, b, core_):
        if m == 0:
            return up.at[mod4(zh + a), mod4(x + b), core_]
        return down.at[mod4(zh + a), mod4(x + b)]

    def piece(m, a, b, p, count=1):
        if m == 0:
            return block(m, a, b, core).at[rows_of(m, a, p, count)]
        return down.at[mod4(zh + a), mod4(x + b), rows_of(m, a, p, count)]

    def z_key(m, a, p):
        return ("z", m, a % 4, p)

    def x_key(m, a, b, p):
        n = pieces(m, a)
        alone = (b % 4 == 3 and p < n // 2) or (b % 4 == 1 and p >= n // 2)
        return ("x", m, a % 4, b % 4, p if alone else "rest")

    def z_send(m, a, p, way):
        step = {"z+": 1, "z-": -1}[way]
        if a == 0:
            rows = rows_of(m, 1, p)
            src = (up_in, down_in)[m].at[rows]
            if m == 0:
                dst = up.at[zh, x, core].at[rows]
            else:
                dst = down.at[zh, x, rows]
        else:
            src = dst = piece(m, a, 0, p)
        send(src, dst, ("z", m), z_key(m, a - step, p), at_seq(step, 0, core))

    def x_send(m, a, b, p, way):
        step = {"x+": 1, "x-": -1}[way]
        src = dst = piece(m, a, b, p)
        if a == 0 and b == 0:
            src = (up_in, down_in)[m].at[rows_of(m, 0, p)]
        send(src, dst, ("x", m), x_key(m, a, b - step, p), at_seq(0, step, core))

    def swap(a, b):
        place = block(0, a, b, core)
        send(up_in if a == 0 and b == 0 else place, place, "s", ("s", a % 4), sibling)

    def z_first(m, i):
        z_send(m, 0, i, "z+")
        z_send(m, 0, pieces(m, 1) - 1 - i, "z-")

    def x_first(m):
        n = pieces(m, 0)
        for i in range(n):
            x_send(m, 0, 0, i, "x+")
            x_send(m, 0, 0, n - 1 - i, "x-")
        if m == 0:
            swap(0, 0)

    def z_piece(m, a, p):
        n = pieces(m, a)
        recv(piece(m, a, 0, p), z_key(m, a, p))
        if a == -1 and p < n // 2:
            z_send(m, a, p, "z+")
        if a == 1 and p >= n // 2:
            z_send(m, a, p, "z-")
        x_send(m, a, 0, p, "x+")
        x_send(m, a, 0, p, "x-")

    def z_far(m, low):
        high = pieces(m, 2) - 1 - low
        for p in (low, high):
            recv(piece(m, 2, 0, p), z_key(m, 2, p))
        x_send(m, 2, 0, low, "x+")
        x_send(m, 2, 0, high, "x-")
        x_send(m, 2, 0, high, "x+")
        x_send(m, 2, 0, low, "x-")

    def x_piece(m, a, b, p):
        recv(piece(m, a, b, p), x_key(m, a, b, p))
        x_send(m, a, b, p, "x+" if b == -1 else "x-")

    def x_rest(m, a, b):
        n = pieces(m, a)
        first, count = {-1: (n // 2, n // 2), 1: (0, n // 2), 2: (0, n)}[b]
        recv(piece(m, a, b, first, count), x_key(m, a, b, first))
        if m == 0:
            swap(a, b)

    def pack():
        for i in (0, 1, 2, 4):
            locals_[i].wait()
        rows_f[:, OWN_VARS * (PIX + 1) :, :] = jnp.zeros((16, ROWS - OWN_VARS * (PIX + 1), HS), F32)
        for j in range(16):
            col = pl.ds(pl.multiple_of(j * COLS + core * HS, HS), HS)
            for v in range(OWN_VARS):
                rows_f[j, v * PIX : (v + 1) * PIX, :] = emb[v, :, col].astype(F32)
            rows_f[j, OWN_VARS * PIX : OWN_VARS * (PIX + 1), :] = bias[:, col].astype(F32)
        for j in range(16):
            tab_out[j % 4, j // 4] = rows_f[j].astype(BF16)
        row = lax.broadcasted_iota(jnp.int32, (ROWS, TOK), 0)
        pix_f[...] = jnp.where(row < OWN_VARS * (PIX + 1), 1.0, 0.0)
        for v in range(OWN_VARS):
            pix_f[v * PIX : (v + 1) * PIX, :] = pix[v].astype(F32)
        for h in range(2):
            pix_f[ROWS - 2 + h : ROWS - 1 + h, :] = query[h * HS : (h + 1) * HS].astype(F32).reshape(1, HS)
        pat[zl, y] = pix_f[...].astype(BF16)
        tab_mid[y] = tab_out[y]

    def start():
        for i in (1, 2, 3):
            send(pat.at[zl, y], pat.at[zl, y], "pz", "pz", at_var(mod4(zl + i), y))
        for i in (1, 3, 2):
            y_ = mod4(y + i)
            send(tab_out.at[y_], tab_mid.at[y], "ty", "ty", at_var(zl, y_))

    def points_y():
        recv(pat.at[0:3, 0], "pz")
        for i in (1, 3, 2):
            send(pat.at[:, y], pat.at[:, y], "py", "py", at_var(zl, mod4(y + i)))

    def table_z():
        recv(tab_mid.at[0:3], "ty")
        for step in (1, -1, 2 - 4 * core):
            send(tab_mid.at[:, x], tab.at[core, x, zl], "tz", "tz", at_z(step))
        tab[core, x, zl] = tab_mid[:, x]

    def table_x():
        recv(tab.at[core, x, 0:3], "tz")
        for b in (1, -1):
            send(tab.at[core, x], tab.at[core, x], "tx", ("tx", -b % 4), at_seq(0, b, core))
        send(tab.at[core, x], tab.at[core, x], "ts", ("ts", 0), sibling)

    def table_swap(b):
        place = tab.at[core, mod4(x + b)]
        recv(place, ("tx", b % 4))
        if b != 2:
            part = place.at[pl.ds(0 if b == -1 else 2, 2)]
            send(part, part, "tx", ("tx", 2), at_seq(0, -b, core))
        send(place, place, "ts", ("ts", b % 4), sibling)

    def aggregate(b):
        quarter = mod4(x + b)
        if b == 0:
            recv(pat.at[0:3], "py")
            locals_[3].wait()
            for ref, dim in ((collect, 1), (expand, 0)):
                which, real = block_of(lax.broadcasted_iota(jnp.int32, ref.shape, dim))
                own = (which == lax.broadcasted_iota(jnp.int32, ref.shape, 1 - dim)) & real
                ref[...] = jnp.where(own, 1.0, 0.0).astype(BF16)
        recv(tab.at[other, quarter], ("ts", b % 4))
        points_f = pat[...].reshape(DEPTH, TOK).astype(F32)
        twice = jnp.concatenate([points_f, points_f], axis=1)
        tables = [tab[h, quarter].reshape(DEPTH, HS) for h in range(2)]
        queries = pat[quarter, y].astype(F32)
        shares = []
        for h in range(2):
            query_f = queries[ROWS - 2 + h : ROWS - 1 + h, :]
            dots = jnp.sum(tables[h].astype(F32) * query_f, axis=1, keepdims=True)
            shares.append((dots * (1.0 / math.sqrt(HS))) * points_f)
        share = jnp.concatenate(shares, axis=1)
        scores = jnp.zeros((N_VARS, COLS), F32)
        for _ in range(3):
            piece = share.astype(BF16)
            share = share - piece.astype(F32)
            scores = scores + jnp.dot(collect[...], piece, preferred_element_type=F32)
        diagonal = lax.broadcasted_iota(jnp.int32, (N_VARS, N_VARS), 0) == lax.broadcasted_iota(
            jnp.int32, (N_VARS, N_VARS), 1
        )
        keep = jnp.sum(
            jnp.where(diagonal, mask[...].astype(F32).reshape(1, N_VARS), 0.0), axis=1, keepdims=True
        )
        scores = jnp.where(keep > 0.0, scores, -1e30)
        expo = jnp.exp(scores - jnp.max(scores, axis=0, keepdims=True))
        weights = (expo / jnp.sum(expo, axis=0, keepdims=True)).astype(BF16)
        mixed = jnp.dot(expand[...], weights, preferred_element_type=F32) * twice
        high = mixed.astype(BF16)
        low = (mixed - high.astype(F32)).astype(BF16)
        over_rows = (((0,), (0,)), ((), ()))
        merged = []
        for h in range(2):
            cols = slice(h * HS, (h + 1) * HS)
            merged.append(
                lax.dot_general(high[:, cols], tables[h], over_rows, preferred_element_type=F32)
                + lax.dot_general(low[:, cols], tables[h], over_rows, preferred_element_type=F32)
            )
        place = agg.at[quarter * 4 + y]
        place[...] = jnp.concatenate(merged, axis=1).astype(BF16)
        for i in (1, 3, 2):
            send(place, place, "agg", "ay", at_var(zl, mod4(y + i)))

    def layer_norm():
        recv(agg.at[0:12], "ay")
        sums = jnp.zeros((TOK, COLS), F32)
        for v in range(16):
            sums = sums + agg[v].astype(F32)
        mean = jnp.sum(sums, axis=1, keepdims=True) * (1.0 / D)
        sums = jnp.zeros((TOK, COLS), F32)
        for v in range(16):
            centered = agg[v].astype(F32) - mean
            sums = sums + centered * centered
        variance = jnp.sum(sums, axis=1, keepdims=True) * (1.0 / D)
        scale = lax.rsqrt(variance + 1e-05)
        locals_[5].wait()
        for v in range(16):
            cols = slice(v * COLS, (v + 1) * COLS)
            gains = gain[cols].astype(F32).reshape(1, COLS)
            norm[v // 4, :, (v % 4) * COLS : (v % 4 + 1) * COLS] = (
                (agg[v].astype(F32) - mean) * scale * gains
            ).astype(BF16)

    def up_part(a):
        if a == 0:
            locals_[6].wait()
        q = mod4(zh + a)
        recv(up.at[q, :, other], ("s", a % 4))
        value = jnp.dot(norm[q], up[q].reshape(1024, FF), preferred_element_type=F32)
        part[...] = value if a == 0 else part[...] + value

    def activate():
        hidden[core] = jax.nn.gelu(part[...], approximate=True).astype(BF16)
        send(hidden.at[core], hidden.at[core], "h", "h", sibling)

    def halves(a):
        n = 2 if a == 2 else 1
        return [slice(i * TOK // n, (i + 1) * TOK // n) for i in range(n)]

    def down_part(a, b):
        if a == 0 and b == 0:
            locals_[7].wait()
            recv(hidden.at[other], "h")
        q, y_ = mod4(zh + a), mod4(x + b)
        away = mod4(y_ - y)
        value = jnp.dot(hidden[...].reshape(2 * TOK, FF), down[q, y_], preferred_element_type=F32)
        term[a % 4, b % 4] = value.astype(BF16).reshape(2, TOK, HS)

        def deliver(core_):
            for half in halves(a):
                src, dst = term.at[a % 4, b % 4, core_, half], got_y.at[a % 4, away * 2 + core, half]
                send(src, dst, "ry", ("ry", a % 4, half.start), (zl * 4 + y_, zh * 8 + x * 2 + core_))

        deliver(other)

        @pl.when(away == 0)
        def _():
            own_sum[a % 4] = term[a % 4, b % 4, core].astype(F32)

        @pl.when(away != 0)
        def _():
            deliver(core)

    def down_sum(a, number=0):
        a, half = a % 4, halves(a)[number]
        q = mod4(zh + a)
        away = mod4(zl - q)
        recv(got_y.at[a, 0:7, half], ("ry", a, half.start))
        for core_ in (core, other):
            cols = pl.ds(pl.multiple_of(core_ * HS, HS), HS)
            value = own_sum[a, half] if core_ is core else got_y[a, other, half].astype(F32)
            for i in (1, 2, 3):
                value = value + got_y[a, i * 2 + core_, half].astype(F32)

            @pl.when(away == 0)
            def _():
                total[half, cols] = value

            summed[a, half, cols] = value.astype(BF16)

        @pl.when(away != 0)
        def _():
            send(summed.at[a, half], got_z.at[away, half], "rz", "rz", at_var(q, y))

    def all_sent():
        for m in (0, 1):
            sent(up.at[0, 0:3, 0], ("z", m))
            sent(up.at[0:3, :, 0], ("x", m))
        sent(up.at[0:2], "s")
        sent(hidden.at[0], "h")
        sent(pat.at[0, 0:3], "pz")
        sent(pat.at[0:3], "py")
        sent(tab_mid.at[0:3], "tz")
        sent(tab_mid.at[0:3], "ty")
        sent(tab.at[0, 0:3], "tx")
        sent(tab.at[0], "ts")
        sent(agg.at[0:12], "agg")

    def finish():
        result = agg[var].astype(F32) + total[...]
        recv(got_z.at[1:4], "rz")
        for i in (1, 2, 3):
            result = result + got_z[i].astype(F32)
        out[...] = result.astype(BF16)
        sent(got_y.at[:, 0:7], "ry")
        sent(got_z.at[0:3], "rz")

    steps = {
        "pack": pack,
        "start": start,
        "z0": lambda i: z_first(0, i),
        "x0": x_first,
        "z1": lambda i: z_first(1, i),
        "Z": z_piece,
        "Z2": z_far,
        "X": x_piece,
        "XR": x_rest,
        "S": swap,
        "py": points_y,
        "tz": table_z,
        "tx": table_x,
        "tsib": table_swap,
        "agg": aggregate,
        "ln": layer_norm,
        "up": up_part,
        "hid": activate,
        "dp": down_part,
        "sent": all_sent,
        "ds": down_sum,
        "fin": finish,
    }
    for name, *rest in ORDER:
        steps[name](*rest)
    assert len(keys) <= N_RECV and len(groups) <= N_SENT


def shards(pixels, w_embed, var_embed, var_mask, agg_query, ln_gain, w_up, w_down):
    vmem = pltpu.VMEM
    return pl.pallas_call(
        kernel,
        out_shape=jax.ShapeDtypeStruct((TOK, COLS), BF16),
        in_specs=[pl.BlockSpec(memory_space=pl.ANY)] * 8,
        out_specs=pl.BlockSpec(memory_space=pltpu.VMEM),
        scratch_shapes=[
            vmem((OWN_VARS, PIX, TOK), BF16),
            vmem((OWN_VARS, PIX, D), BF16),
            vmem((OWN_VARS, D), BF16),
            vmem((N_VARS,), jnp.int32),
            vmem((COLS,), BF16),
            vmem((D,), BF16),
            vmem((16, ROWS, HS), F32),
            vmem((ROWS, TOK), F32),
            vmem((4, 4, ROWS, HS), BF16),
            vmem((4, 4, ROWS, HS), BF16),
            vmem((2, 4, 4, 4, ROWS, HS), BF16),
            vmem((N_VARS, DEPTH), BF16),
            vmem((DEPTH, N_VARS), BF16),
            vmem((4, 4, ROWS, TOK), BF16),
            vmem((16, TOK, COLS), BF16),
            vmem((4, TOK, 1024), BF16),
            vmem((4, 4, 2, 128, FF), BF16),
            vmem((4, 4, FF, HS), BF16),
            vmem((4, TOK, HS), F32),
            vmem((4, 4, 2, TOK, HS), BF16),
            vmem((4, 8, TOK, HS), BF16),
            vmem((4, TOK, COLS), BF16),
            vmem((4, TOK, COLS), BF16),
            vmem((2, TOK, FF), BF16),
            vmem((TOK, FF), F32),
            vmem((TOK, COLS), F32),
            pltpu.SemaphoreType.DMA((8,)),
            pltpu.SemaphoreType.DMA((N_SENT,)),
            pltpu.SemaphoreType.DMA((N_RECV,)),
        ],
        compiler_params=pltpu.CompilerParams(
            collective_id=0, has_side_effects=True, vmem_limit_bytes=56 * 1024 * 1024
        ),
    )(pixels, w_embed, var_embed, var_mask, agg_query, ln_gain, w_up, w_down)


def solution(mesh):
    return jax.shard_map(
        shards,
        mesh=mesh,
        in_specs=(
            P("var", None, "seq"),
            P("var", None, None),
            P("var", None),
            P(),
            P("var"),
            P(),
            P("seq", "var"),
            P("var", "seq"),
        ),
        out_specs=P("seq", "var"),
        check_vma=False,
    )
```

```python
import math

import jax
import jax.numpy as jnp
from jax import lax
from jax.experimental import pallas as pl
from jax.experimental.pallas import tpu as pltpu
from jax.sharding import PartitionSpec as P

MESH = pl.DeviceIdType.MESH
F32, BF16 = jnp.float32, jnp.bfloat16
PIX, HS = 4, 128
N_VARS = 96
OWN_VARS = 6
ROWS = 32
DEPTH = 16 * ROWS
TOK, COLS, D, FF = 128, 256, 4096, 512
N_SENT, N_RECV = 15, 99
SPLIT = (4, 4)
SPLIT_NEAR = (2, 2)
ORDER = (
    ("pack",), ("start",), ("z0", 0), ("z0", 1), ("tz",), ("z0", 2), ("x0", 0), ("z0", 3), ("py",), ("x0", 1),
    ("Z", 0, -1, 1), ("Z", 0, 1, 3), ("X", 0, 0, -1, 0), ("XR", 0, 0, -1), ("Z", 0, 1, 2), ("tx",), ("Z", 0, -1, 0),
    ("X", 0, 0, 1, 1), ("agg", 0), ("Z", 0, 1, 1), ("X", 0, 1, 1, 3), ("XR", 0, 0, 1), ("X", 1, 0, -1, 0), ("z1", 0),
    ("tsib", 1), ("z1", 1), ("Z", 0, 1, 0), ("tsib", -1), ("Z", 0, -1, 2), ("agg", -1), ("z1", 2), ("X", 0, 1, 1, 2),
    ("X", 0, 1, -1, 1), ("Z", 0, -1, 3), ("Z2", 0, 0), ("agg", 1), ("z1", 3), ("X", 1, 0, 1, 1), ("Z2", 0, 1),
    ("X", 0, -1, 1, 2), ("tsib", 2), ("S", -1, 0), ("XR", 0, 0, 2), ("X", 0, -1, -1, 0), ("agg", 2),
    ("X", 0, 2, -1, 0), ("X", 0, 2, -1, 1), ("XR", 0, 1, 1), ("Z", 1, -1, 0), ("X", 0, -1, -1, 1), ("S", 2, 0),
    ("XR", 0, -1, -1), ("X", 0, 2, 1, 3), ("X", 0, -1, 1, 3), ("X", 0, 2, 1, 2), ("X", 0, 1, -1, 0), ("S", 1, 0),
    ("XR", 0, 1, -1), ("Z", 1, 1, 3), ("Z", 1, -1, 2), ("Z", 1, -1, 1), ("Z", 1, 1, 1), ("ln",), ("XR", 0, 1, 2),
    ("XR", 0, -1, 1), ("Z", 1, 1, 2), ("XR", 1, 0, 2), ("X", 1, -1, -1, 0), ("XR", 0, 2, 2), ("XR", 0, -1, 2),
    ("XR", 1, 0, -1), ("up", 0), ("XR", 0, 2, 1), ("up", 1), ("Z", 1, -1, 3), ("XR", 0, 2, -1), ("X", 1, -1, -1, 1),
    ("up", -1), ("X", 1, -1, 1, 2), ("up", 2), ("X", 1, 1, 1, 3), ("hid",), ("Z", 1, 1, 0), ("dp", 0, 0),
    ("dp", 1, 0), ("X", 1, -1, 1, 3), ("XR", 1, 0, 1), ("X", 1, 1, 1, 2), ("dp", -1, 0), ("X", 1, 1, -1, 1),
    ("Z2", 1, 0), ("XR", 1, -1, -1), ("X", 1, 1, -1, 0), ("dp", 0, 1), ("Z2", 1, 1), ("dp", -1, -1), ("XR", 1, 1, -1),
    ("dp", 0, 2), ("XR", 1, -1, 2), ("XR", 1, 1, 1), ("dp", 0, -1), ("dp", -1, 2), ("X", 1, 2, 1, 3),
    ("XR", 1, -1, 1), ("dp", 1, -1), ("dp", -1, 1), ("X", 1, 2, -1, 0), ("X", 1, 2, -1, 1), ("XR", 1, 1, 2),
    ("X", 1, 2, 1, 2), ("dp", 1, 1), ("dp", 1, 2), ("XR", 1, 2, 1), ("dp", 2, 1), ("dp", 2, 0), ("XR", 1, 2, -1),
    ("ds", 0), ("dp", 2, -1), ("XR", 1, 2, 2), ("dp", 2, 2), ("ds", -1), ("ds", 1), ("ds", 2, 0), ("sent",),
    ("ds", 2, 1), ("fin",),
)


def block_of(iota):
    owner, row = iota // ROWS, iota % ROWS
    local = jnp.where(row < OWN_VARS * PIX, row // PIX, row - OWN_VARS * PIX)
    return owner * OWN_VARS + local, row < OWN_VARS * (PIX + 1)


def kernel(
    pix_in, emb_in, bias_in, mask_in, query_in, gain_in, up_in, down_in, out,
    pix, emb, bias, mask, query, gain, rows_f, pix_f,
    tab_out, tab_mid, tab, collect, expand, pat, agg, norm, up, down, own_sum, term, got_y, got_z, summed, hidden, part, total,
    local_sem, send_sem, recv_sem,
):
    var, seq = lax.axis_index("var"), lax.axis_index("seq")
    zl, y = var // 4, lax.rem(var, 4)
    zh, x, core = seq // 8, lax.rem(seq // 2, 4), lax.rem(seq, 2)
    z = zh * 4 + zl
    other = 1 - core

    def mod4(v):
        return lax.rem(v + 4, 4)

    def at_var(zl_, y_):
        return (zl_ * 4 + y_, seq)

    def at_seq(a, b, core_):
        return (var, mod4(zh + a) * 8 + mod4(x + b) * 2 + core_)

    def at_z(d):
        z_ = lax.rem(z + d + 16, 16)
        return (lax.rem(z_, 4) * 4 + y, (z_ // 4) * 8 + x * 2 + core)

    sibling = at_seq(0, 0, other)

    barrier = pltpu.get_barrier_semaphore()
    peers = [at_z(1), at_z(-1), at_z(2), at_z(-2), sibling]
    peers += [at_var(mod4(zl + i), y) for i in (1, 2, 3)]
    peers += [at_var(zl, mod4(y + i)) for i in (1, 2, 3)]
    peers += [at_seq(1, 0, core), at_seq(-1, 0, core)]
    peers += [at_seq(0, i, core) for i in (1, 3)]
    for peer in peers:
        pl.semaphore_signal(barrier, inc=1, device_id=peer, device_id_type=MESH)

    locals_ = []
    for i, (src, dst) in enumerate(
        (
            (pix_in, pix),
            (emb_in, emb),
            (bias_in, bias),
            (mask_in, mask),
            (query_in, query),
            (gain_in, gain),
            (up_in, up.at[zh, x, core]),
            (down_in, down.at[zh, x]),
        )
    ):
        locals_.append(pltpu.make_async_copy(src, dst, local_sem.at[i]))
        locals_[-1].start()

    groups, keys = {}, {}

    def sem_of(key):
        return keys.setdefault(key, len(keys))

    def copy_of(src, dst, group, key, device):
        return pltpu.make_async_remote_copy(
            src_ref=src,
            dst_ref=dst,
            send_sem=send_sem.at[groups.setdefault(group, len(groups))],
            recv_sem=recv_sem.at[sem_of(key)],
            device_id=device,
            device_id_type=MESH,
        )

    def send(src, dst, group, key, device):
        copy_of(src, dst, group, key, device).start()

    def recv(view, key):
        copy_of(view, view, next(iter(groups)), key, sibling).wait_recv()

    def sent(view, group):
        copy_of(view, view, group, next(iter(keys)), sibling).wait_send()

    pl.semaphore_wait(barrier, len(peers))


    def pieces(m, a):
        return (SPLIT if a % 4 else SPLIT_NEAR)[m]

    def rows_of(m, a, p, count=1):
        n = (HS, FF)[m] // pieces(m, a)
        return pl.ds(p * n, n * count)

    def block(m, a, b, core_):
        if m == 0:
            return up.at[mod4(zh + a), mod4(x + b), core_]
        return down.at[mod4(zh + a), mod4(x + b)]

    def piece(m, a, b, p, count=1):
        if m == 0:
            return block(m, a, b, core).at[rows_of(m, a, p, count)]
        return down.at[mod4(zh + a), mod4(x + b), rows_of(m, a, p, count)]

    def z_key(m, a, p):
        return ("z", m, a % 4, p)

    def x_key(m, a, b, p):
        n = pieces(m, a)
        alone = (b % 4 == 3 and p < n // 2) or (b % 4 == 1 and p >= n // 2)
        return ("x", m, a % 4, b % 4, p if alone else "rest")

    def z_send(m, a, p, way):
        step = {"z+": 1, "z-": -1}[way]
        if a == 0:
            rows = rows_of(m, 1, p)
            src = (up_in, down_in)[m].at[rows]
            if m == 0:
                dst = up.at[zh, x, core].at[rows]
            else:
                dst = down.at[zh, x, rows]
        else:
            src = dst = piece(m, a, 0, p)
        send(src, dst, ("z", m), z_key(m, a - step, p), at_seq(step, 0, core))

    def x_send(m, a, b, p, way):
        step = {"x+": 1, "x-": -1}[way]
        src = dst = piece(m, a, b, p)
        if a == 0 and b == 0:
            src = (up_in, down_in)[m].at[rows_of(m, 0, p)]
        send(src, dst, ("x", m), x_key(m, a, b - step, p), at_seq(0, step, core))

    def swap(a, b):
        place = block(0, a, b, core)
        send(up_in if a == 0 and b == 0 else place, place, "s", ("s", a % 4), sibling)

    def z_first(m, i):
        z_send(m, 0, i, "z+")
        z_send(m, 0, pieces(m, 1) - 1 - i, "z-")

    def x_first(m):
        n = pieces(m, 0)
        for i in range(n):
            x_send(m, 0, 0, i, "x+")
            x_send(m, 0, 0, n - 1 - i, "x-")
        if m == 0:
            swap(0, 0)

    def z_piece(m, a, p):
        n = pieces(m, a)
        recv(piece(m, a, 0, p), z_key(m, a, p))
        if a == -1 and p < n // 2:
            z_send(m, a, p, "z+")
        if a == 1 and p >= n // 2:
            z_send(m, a, p, "z-")
        x_send(m, a, 0, p, "x+")
        x_send(m, a, 0, p, "x-")

    def z_far(m, low):
        high = pieces(m, 2) - 1 - low
        for p in (low, high):
            recv(piece(m, 2, 0, p), z_key(m, 2, p))
        x_send(m, 2, 0, low, "x+")
        x_send(m, 2, 0, high, "x-")
        x_send(m, 2, 0, high, "x+")
        x_send(m, 2, 0, low, "x-")

    def x_piece(m, a, b, p):
        recv(piece(m, a, b, p), x_key(m, a, b, p))
        x_send(m, a, b, p, "x+" if b == -1 else "x-")

    def x_rest(m, a, b):
        n = pieces(m, a)
        first, count = {-1: (n // 2, n // 2), 1: (0, n // 2), 2: (0, n)}[b]
        recv(piece(m, a, b, first, count), x_key(m, a, b, first))
        if m == 0:
            swap(a, b)

    def pack():
        for i in (0, 1, 2, 4):
            locals_[i].wait()
        rows_f[:, OWN_VARS * (PIX + 1) :, :] = jnp.zeros((16, ROWS - OWN_VARS * (PIX + 1), HS), F32)
        for j in range(16):
            col = pl.ds(pl.multiple_of(j * COLS + core * HS, HS), HS)
            for v in range(OWN_VARS):
                rows_f[j, v * PIX : (v + 1) * PIX, :] = emb[v, :, col].astype(F32)
            rows_f[j, OWN_VARS * PIX : OWN_VARS * (PIX + 1), :] = bias[:, col].astype(F32)
        for j in range(16):
            tab_out[j % 4, j // 4] = rows_f[j].astype(BF16)
        row = lax.broadcasted_iota(jnp.int32, (ROWS, TOK), 0)
        pix_f[...] = jnp.where(row < OWN_VARS * (PIX + 1), 1.0, 0.0)
        for v in range(OWN_VARS):
            pix_f[v * PIX : (v + 1) * PIX, :] = pix[v].astype(F32)
        for h in range(2):
            pix_f[ROWS - 2 + h : ROWS - 1 + h, :] = query[h * HS : (h + 1) * HS].astype(F32).reshape(1, HS)
        pat[zl, y] = pix_f[...].astype(BF16)
        tab_mid[y] = tab_out[y]

    def start():
        for i in (1, 2, 3):
            send(pat.at[zl, y], pat.at[zl, y], "pz", "pz", at_var(mod4(zl + i), y))
        for i in (1, 3, 2):
            y_ = mod4(y + i)
            send(tab_out.at[y_], tab_mid.at[y], "ty", "ty", at_var(zl, y_))

    def points_y():
        recv(pat.at[0:3, 0], "pz")
        for i in (1, 3, 2):
            send(pat.at[:, y], pat.at[:, y], "py", "py", at_var(zl, mod4(y + i)))

    def table_z():
        recv(tab_mid.at[0:3], "ty")
        for step in (1, -1, 2 - 4 * core):
            send(tab_mid.at[:, x], tab.at[core, x, zl], "tz", "tz", at_z(step))
        tab[core, x, zl] = tab_mid[:, x]

    def table_x():
        recv(tab.at[core, x, 0:3], "tz")
        for b in (1, -1):
            send(tab.at[core, x], tab.at[core, x], "tx", ("tx", -b % 4), at_seq(0, b, core))
        send(tab.at[core, x], tab.at[core, x], "ts", ("ts", 0), sibling)

    def table_swap(b):
        place = tab.at[core, mod4(x + b)]
        recv(place, ("tx", b % 4))
        if b != 2:
            part = place.at[pl.ds(0 if b == -1 else 2, 2)]
            send(part, part, "tx", ("tx", 2), at_seq(0, -b, core))
        send(place, place, "ts", ("ts", b % 4), sibling)

    def aggregate(b):
        quarter = mod4(x + b)
        if b == 0:
            recv(pat.at[0:3], "py")
            locals_[3].wait()
            for ref, dim in ((collect, 1), (expand, 0)):
                which, real = block_of(lax.broadcasted_iota(jnp.int32, ref.shape, dim))
                own = (which == lax.broadcasted_iota(jnp.int32, ref.shape, 1 - dim)) & real
                ref[...] = jnp.where(own, 1.0, 0.0).astype(BF16)
        recv(tab.at[other, quarter], ("ts", b % 4))
        points_f = pat[...].reshape(DEPTH, TOK).astype(F32)
        twice = jnp.concatenate([points_f, points_f], axis=1)
        tables = [tab[h, quarter].reshape(DEPTH, HS) for h in range(2)]
        queries = pat[quarter, y].astype(F32)
        shares = []
        for h in range(2):
            query_f = queries[ROWS - 2 + h : ROWS - 1 + h, :]
            dots = jnp.sum(tables[h].astype(F32) * query_f, axis=1, keepdims=True)
            shares.append((dots * (1.0 / math.sqrt(HS))) * points_f)
        share = jnp.concatenate(shares, axis=1)
        scores = jnp.zeros((N_VARS, COLS), F32)
        for _ in range(3):
            piece = share.astype(BF16)
            share = share - piece.astype(F32)
            scores = scores + jnp.dot(collect[...], piece, preferred_element_type=F32)
        diagonal = lax.broadcasted_iota(jnp.int32, (N_VARS, N_VARS), 0) == lax.broadcasted_iota(
            jnp.int32, (N_VARS, N_VARS), 1
        )
        keep = jnp.sum(
            jnp.where(diagonal, mask[...].astype(F32).reshape(1, N_VARS), 0.0), axis=1, keepdims=True
        )
        scores = jnp.where(keep > 0.0, scores, -1e30)
        expo = jnp.exp(scores - jnp.max(scores, axis=0, keepdims=True))
        weights = (expo / jnp.sum(expo, axis=0, keepdims=True)).astype(BF16)
        mixed = jnp.dot(expand[...], weights, preferred_element_type=F32) * twice
        high = mixed.astype(BF16)
        low = (mixed - high.astype(F32)).astype(BF16)
        over_rows = (((0,), (0,)), ((), ()))
        merged = []
        for h in range(2):
            cols = slice(h * HS, (h + 1) * HS)
            merged.append(
                lax.dot_general(high[:, cols], tables[h], over_rows, preferred_element_type=F32)
                + lax.dot_general(low[:, cols], tables[h], over_rows, preferred_element_type=F32)
            )
        place = agg.at[quarter * 4 + y]
        place[...] = jnp.concatenate(merged, axis=1).astype(BF16)
        for i in (1, 3, 2):
            send(place, place, "agg", "ay", at_var(zl, mod4(y + i)))

    def layer_norm():
        recv(agg.at[0:12], "ay")
        sums = jnp.zeros((TOK, COLS), F32)
        for v in range(16):
            sums = sums + agg[v].astype(F32)
        mean = jnp.sum(sums, axis=1, keepdims=True) * (1.0 / D)
        sums = jnp.zeros((TOK, COLS), F32)
        for v in range(16):
            centered = agg[v].astype(F32) - mean
            sums = sums + centered * centered
        variance = jnp.sum(sums, axis=1, keepdims=True) * (1.0 / D)
        scale = lax.rsqrt(variance + 1e-05)
        locals_[5].wait()
        for v in range(16):
            cols = slice(v * COLS, (v + 1) * COLS)
            gains = gain[cols].astype(F32).reshape(1, COLS)
            norm[v // 4, :, (v % 4) * COLS : (v % 4 + 1) * COLS] = (
                (agg[v].astype(F32) - mean) * scale * gains
            ).astype(BF16)

    def up_part(a):
        if a == 0:
            locals_[6].wait()
        q = mod4(zh + a)
        recv(up.at[q, :, other], ("s", a % 4))
        value = jnp.dot(norm[q], up[q].reshape(1024, FF), preferred_element_type=F32)
        part[...] = value if a == 0 else part[...] + value

    def activate():
        hidden[core] = jax.nn.gelu(part[...], approximate=True).astype(BF16)
        send(hidden.at[core], hidden.at[core], "h", "h", sibling)

    def halves(a):
        n = 2 if a == 2 else 1
        return [slice(i * TOK // n, (i + 1) * TOK // n) for i in range(n)]

    def down_part(a, b):
        if a == 0 and b == 0:
            locals_[7].wait()
            recv(hidden.at[other], "h")
        q, y_ = mod4(zh + a), mod4(x + b)
        away = mod4(y_ - y)
        value = jnp.dot(hidden[...].reshape(2 * TOK, FF), down[q, y_], preferred_element_type=F32)
        term[a % 4, b % 4] = value.astype(BF16).reshape(2, TOK, HS)

        def deliver(core_):
            for half in halves(a):
                src, dst = term.at[a % 4, b % 4, core_, half], got_y.at[a % 4, away * 2 + core, half]
                send(src, dst, "ry", ("ry", a % 4, half.start), (zl * 4 + y_, zh * 8 + x * 2 + core_))

        deliver(other)

        @pl.when(away == 0)
        def _():
            own_sum[a % 4] = term[a % 4, b % 4, core].astype(F32)

        @pl.when(away != 0)
        def _():
            deliver(core)

    def down_sum(a, number=0):
        a, half = a % 4, halves(a)[number]
        q = mod4(zh + a)
        away = mod4(zl - q)
        recv(got_y.at[a, 0:7, half], ("ry", a, half.start))
        for core_ in (core, other):
            cols = pl.ds(pl.multiple_of(core_ * HS, HS), HS)
            value = own_sum[a, half] if core_ is core else got_y[a, other, half].astype(F32)
            for i in (1, 2, 3):
                value = value + got_y[a, i * 2 + core_, half].astype(F32)

            @pl.when(away == 0)
            def _():
                total[half, cols] = value

            summed[a, half, cols] = value.astype(BF16)

        @pl.when(away != 0)
        def _():
            send(summed.at[a, half], got_z.at[away, half], "rz", "rz", at_var(q, y))

    def all_sent():
        for m in (0, 1):
            sent(up.at[0, 0:3, 0], ("z", m))
            sent(up.at[0:3, :, 0], ("x", m))
        sent(up.at[0:2], "s")
        sent(hidden.at[0], "h")
        sent(pat.at[0, 0:3], "pz")
        sent(pat.at[0:3], "py")
        sent(tab_mid.at[0:3], "tz")
        sent(tab_mid.at[0:3], "ty")
        sent(tab.at[0, 0:3], "tx")
        sent(tab.at[0], "ts")
        sent(agg.at[0:12], "agg")

    def finish():
        result = agg[var].astype(F32) + total[...]
        recv(got_z.at[1:4], "rz")
        for i in (1, 2, 3):
            result = result + got_z[i].astype(F32)
        out[...] = result.astype(BF16)
        sent(got_y.at[:, 0:7], "ry")
        sent(got_z.at[0:3], "rz")

    steps = {
        "pack": pack,
        "start": start,
        "z0": lambda i: z_first(0, i),
        "x0": x_first,
        "z1": lambda i: z_first(1, i),
        "Z": z_piece,
        "Z2": z_far,
        "X": x_piece,
        "XR": x_rest,
        "S": swap,
        "py": points_y,
        "tz": table_z,
        "tx": table_x,
        "tsib": table_swap,
        "agg": aggregate,
        "ln": layer_norm,
        "up": up_part,
        "hid": activate,
        "dp": down_part,
        "sent": all_sent,
        "ds": down_sum,
        "fin": finish,
    }
    for name, *rest in ORDER:
        steps[name](*rest)
    assert len(keys) <= N_RECV and len(groups) <= N_SENT


def shards(pixels, w_embed, var_embed, var_mask, agg_query, ln_gain, w_up, w_down):
    vmem = pltpu.VMEM
    return pl.pallas_call(
        kernel,
        out_shape=jax.ShapeDtypeStruct((TOK, COLS), BF16),
        in_specs=[pl.BlockSpec(memory_space=pl.ANY)] * 8,
        out_specs=pl.BlockSpec(memory_space=pltpu.VMEM),
        scratch_shapes=[
            vmem((OWN_VARS, PIX, TOK), BF16),
            vmem((OWN_VARS, PIX, D), BF16),
            vmem((OWN_VARS, D), BF16),
            vmem((N_VARS,), jnp.int32),
            vmem((COLS,), BF16),
            vmem((D,), BF16),
            vmem((16, ROWS, HS), F32),
            vmem((ROWS, TOK), F32),
            vmem((4, 4, ROWS, HS), BF16),
            vmem((4, 4, ROWS, HS), BF16),
            vmem((2, 4, 4, 4, ROWS, HS), BF16),
            vmem((N_VARS, DEPTH), BF16),
            vmem((DEPTH, N_VARS), BF16),
            vmem((4, 4, ROWS, TOK), BF16),
            vmem((16, TOK, COLS), BF16),
            vmem((4, TOK, 1024), BF16),
            vmem((4, 4, 2, 128, FF), BF16),
            vmem((4, 4, FF, HS), BF16),
            vmem((4, TOK, HS), F32),
            vmem((4, 4, 2, TOK, HS), BF16),
            vmem((4, 8, TOK, HS), BF16),
            vmem((4, TOK, COLS), BF16),
            vmem((4, TOK, COLS), BF16),
            vmem((2, TOK, FF), BF16),
            vmem((TOK, FF), F32),
            vmem((TOK, COLS), F32),
            pltpu.SemaphoreType.DMA((8,)),
            pltpu.SemaphoreType.DMA((N_SENT,)),
            pltpu.SemaphoreType.DMA((N_RECV,)),
        ],
        compiler_params=pltpu.CompilerParams(
            collective_id=0, has_side_effects=True, vmem_limit_bytes=56 * 1024 * 1024
        ),
    )(pixels, w_embed, var_embed, var_mask, agg_query, ln_gain, w_up, w_down)


def solution(mesh):
    return jax.shard_map(
        shards,
        mesh=mesh,
        in_specs=(
            P("var", None, "seq"),
            P("var", None, None),
            P("var", None),
            P(),
            P("var"),
            P(),
            P("seq", "var"),
            P("var", "seq"),
        ),
        out_specs=P("seq", "var"),
        check_vma=False,
    )
```

```python
import math

import jax
import jax.numpy as jnp
from jax import lax
from jax.experimental import pallas as pl
from jax.experimental.pallas import tpu as pltpu
from jax.sharding import PartitionSpec as P

MESH = pl.DeviceIdType.MESH
F32, BF16 = jnp.float32, jnp.bfloat16
PIX, HS = 4, 128
N_VARS = 96
OWN_VARS = 6
ROWS = 32
DEPTH = 16 * ROWS
TOK, COLS, D, FF = 128, 256, 4096, 512
N_SENT, N_RECV = 15, 99
SPLIT = (4, 4)
SPLIT_NEAR = (2, 2)
ORDER = (
    ("x0", 0), ("z0", 0), ("pack",), ("z0", 1), ("start",), ("x0", 1), ("tz",), ("z0", 2), ("X", 0, 0, 1, 1),
    ("X", 1, 0, -1, 0), ("Z", 0, 1, 3), ("py",), ("z0", 3), ("Z", 0, -1, 0), ("X", 1, 0, 1, 1), ("tx",),
    ("X", 0, 0, -1, 0), ("XR", 0, 0, 1), ("Z", 0, -1, 1), ("Z", 0, 1, 2), ("X", 0, 1, 1, 3), ("agg", 0),
    ("XR", 1, 0, 1), ("z1", 0), ("Z", 0, 1, 1), ("tsib", 1), ("tsib", -1), ("Z", 0, -1, 3), ("X", 0, -1, -1, 0),
    ("agg", -1), ("Z", 0, -1, 2), ("XR", 0, 0, -1), ("X", 0, -1, -1, 1), ("z1", 1), ("Z", 0, 1, 0), ("z1", 2),
    ("X", 0, 1, -1, 1), ("agg", 1), ("tsib", 2), ("Z2", 0, 1), ("z1", 3), ("X", 0, 1, 1, 2), ("Z2", 0, 0), ("agg", 2),
    ("XR", 0, 0, 2), ("X", 0, -1, 1, 3), ("Z", 1, 1, 3), ("X", 0, 1, -1, 0), ("S", -1, 0), ("X", 0, -1, 1, 2),
    ("X", 0, 2, -1, 0), ("X", 0, 2, 1, 3), ("X", 0, 2, -1, 1), ("S", 1, 0), ("X", 0, 2, 1, 2), ("Z", 1, 1, 1),
    ("XR", 0, 1, -1), ("XR", 1, 0, -1), ("Z", 1, -1, 0), ("ln",), ("Z", 1, -1, 1), ("XR", 1, 0, 2), ("XR", 0, 2, 1),
    ("S", 2, 0), ("XR", 0, 1, 2), ("XR", 0, -1, -1), ("XR", 0, -1, 1), ("Z", 1, 1, 2), ("XR", 0, 2, 2),
    ("Z", 1, -1, 2), ("XR", 0, 1, 1), ("XR", 0, 2, -1), ("Z", 1, -1, 3), ("up", 0), ("Z", 1, 1, 0), ("XR", 0, -1, 2),
    ("up", 1), ("up", 2), ("up", -1), ("hid",), ("X", 1, -1, -1, 1), ("X", 1, 1, 1, 3), ("Z2", 1, 0), ("dp", 0, 0),
    ("X", 1, -1, -1, 0), ("X", 1, 1, -1, 1), ("X", 1, -1, 1, 2), ("dp", -1, 0), ("X", 1, -1, 1, 3), ("dp", 0, 2),
    ("dp", 0, 1), ("dp", 1, 0), ("Z2", 1, 1), ("X", 1, 1, -1, 0), ("X", 1, 1, 1, 2), ("dp", 2, 0), ("dp", 0, -1),
    ("XR", 1, -1, -1), ("XR", 1, -1, 1), ("X", 1, 2, 1, 3), ("X", 1, 2, -1, 0), ("XR", 1, 1, -1), ("XR", 1, 1, 1),
    ("dp", -1, 1), ("dp", -1, -1), ("XR", 1, -1, 2), ("dp", -1, 2), ("dp", 1, 1), ("X", 1, 2, -1, 1),
    ("X", 1, 2, 1, 2), ("dp", 1, -1), ("XR", 1, 2, -1), ("XR", 1, 1, 2), ("dp", 1, 2), ("dp", 2, -1), ("XR", 1, 2, 1),
    ("XR", 1, 2, 2), ("ds", 0), ("dp", 2, 2), ("dp", 2, 1), ("ds", -1), ("ds", 1), ("ds", 2, 0), ("sent",),
    ("ds", 2, 1), ("fin",),
)


def block_of(iota):
    owner, row = iota // ROWS, iota % ROWS
    local = jnp.where(row < OWN_VARS * PIX, row // PIX, row - OWN_VARS * PIX)
    return owner * OWN_VARS + local, row < OWN_VARS * (PIX + 1)


def kernel(
    pix_in, emb_in, bias_in, mask_in, query_in, gain_in, up_in, down_in, out,
    pix, emb, bias, mask, query, gain, rows_f, pix_f,
    tab_out, tab_mid, tab, collect, expand, pat, agg, norm, up, down, own_sum, term, got_y, got_z, summed, hidden, part, total,
    local_sem, send_sem, recv_sem,
):
    var, seq = lax.axis_index("var"), lax.axis_index("seq")
    zl, y = var // 4, lax.rem(var, 4)
    zh, x, core = seq // 8, lax.rem(seq // 2, 4), lax.rem(seq, 2)
    z = zh * 4 + zl
    other = 1 - core

    def mod4(v):
        return lax.rem(v + 4, 4)

    def at_var(zl_, y_):
        return (zl_ * 4 + y_, seq)

    def at_seq(a, b, core_):
        return (var, mod4(zh + a) * 8 + mod4(x + b) * 2 + core_)

    def at_z(d):
        z_ = lax.rem(z + d + 16, 16)
        return (lax.rem(z_, 4) * 4 + y, (z_ // 4) * 8 + x * 2 + core)

    sibling = at_seq(0, 0, other)

    barrier = pltpu.get_barrier_semaphore()
    peers = [at_z(1), at_z(-1), at_z(2), at_z(-2), sibling]
    peers += [at_var(mod4(zl + i), y) for i in (1, 2, 3)]
    peers += [at_var(zl, mod4(y + i)) for i in (1, 2, 3)]
    peers += [at_seq(1, 0, core), at_seq(-1, 0, core)]
    peers += [at_seq(0, i, core) for i in (1, 3)]
    for peer in peers:
        pl.semaphore_signal(barrier, inc=1, device_id=peer, device_id_type=MESH)

    locals_ = []
    for i, (src, dst) in enumerate(
        (
            (pix_in, pix),
            (emb_in, emb),
            (bias_in, bias),
            (mask_in, mask),
            (query_in, query),
            (gain_in, gain),
            (up_in, up.at[zh, x, core]),
            (down_in, down.at[zh, x]),
        )
    ):
        locals_.append(pltpu.make_async_copy(src, dst, local_sem.at[i]))
        locals_[-1].start()

    groups, keys = {}, {}

    def sem_of(key):
        return keys.setdefault(key, len(keys))

    def copy_of(src, dst, group, key, device):
        return pltpu.make_async_remote_copy(
            src_ref=src,
            dst_ref=dst,
            send_sem=send_sem.at[groups.setdefault(group, len(groups))],
            recv_sem=recv_sem.at[sem_of(key)],
            device_id=device,
            device_id_type=MESH,
        )

    def send(src, dst, group, key, device):
        copy_of(src, dst, group, key, device).start()

    def recv(view, key):
        copy_of(view, view, next(iter(groups)), key, sibling).wait_recv()

    def sent(view, group):
        copy_of(view, view, group, next(iter(keys)), sibling).wait_send()

    pl.semaphore_wait(barrier, len(peers))
    for i in (6, 7):
        locals_[i].wait()


    def pieces(m, a):
        return (SPLIT if a % 4 else SPLIT_NEAR)[m]

    def rows_of(m, a, p, count=1):
        n = (HS, FF)[m] // pieces(m, a)
        return pl.ds(p * n, n * count)

    def block(m, a, b, core_):
        if m == 0:
            return up.at[mod4(zh + a), mod4(x + b), core_]
        return down.at[mod4(zh + a), mod4(x + b)]

    def piece(m, a, b, p, count=1):
        if m == 0:
            return block(m, a, b, core).at[rows_of(m, a, p, count)]
        return down.at[mod4(zh + a), mod4(x + b), rows_of(m, a, p, count)]

    def z_key(m, a, p):
        return ("z", m, a % 4, p)

    def x_key(m, a, b, p):
        n = pieces(m, a)
        alone = (b % 4 == 3 and p < n // 2) or (b % 4 == 1 and p >= n // 2)
        return ("x", m, a % 4, b % 4, p if alone else "rest")

    def z_send(m, a, p, way):
        step = {"z+": 1, "z-": -1}[way]
        if a == 0:
            rows = rows_of(m, 1, p)
            if m == 0:
                src = dst = up.at[zh, x, core].at[rows]
            else:
                src = dst = down.at[zh, x, rows]
        else:
            src = dst = piece(m, a, 0, p)
        send(src, dst, ("z", m), z_key(m, a - step, p), at_seq(step, 0, core))

    def x_send(m, a, b, p, way):
        step = {"x+": 1, "x-": -1}[way]
        src = dst = piece(m, a, b, p)
        send(src, dst, ("x", m), x_key(m, a, b - step, p), at_seq(0, step, core))

    def swap(a, b):
        place = block(0, a, b, core)
        send(place, place, "s", ("s", a % 4), sibling)

    def z_first(m, i):
        z_send(m, 0, i, "z+")
        z_send(m, 0, pieces(m, 1) - 1 - i, "z-")

    def x_first(m):
        n = pieces(m, 0)
        for i in range(n):
            x_send(m, 0, 0, i, "x+")
            x_send(m, 0, 0, n - 1 - i, "x-")
        if m == 0:
            swap(0, 0)

    def z_piece(m, a, p):
        n = pieces(m, a)
        recv(piece(m, a, 0, p), z_key(m, a, p))
        if a == -1 and p < n // 2:
            z_send(m, a, p, "z+")
        if a == 1 and p >= n // 2:
            z_send(m, a, p, "z-")
        x_send(m, a, 0, p, "x+")
        x_send(m, a, 0, p, "x-")

    def z_far(m, low):
        high = pieces(m, 2) - 1 - low
        for p in (low, high):
            recv(piece(m, 2, 0, p), z_key(m, 2, p))
        x_send(m, 2, 0, low, "x+")
        x_send(m, 2, 0, high, "x-")
        x_send(m, 2, 0, high, "x+")
        x_send(m, 2, 0, low, "x-")

    def x_piece(m, a, b, p):
        recv(piece(m, a, b, p), x_key(m, a, b, p))
        x_send(m, a, b, p, "x+" if b == -1 else "x-")

    def x_rest(m, a, b):
        n = pieces(m, a)
        first, count = {-1: (n // 2, n // 2), 1: (0, n // 2), 2: (0, n)}[b]
        recv(piece(m, a, b, first, count), x_key(m, a, b, first))
        if m == 0:
            swap(a, b)

    def pack():
        for i in (0, 1, 2, 4):
            locals_[i].wait()
        rows_f[:, OWN_VARS * (PIX + 1) :, :] = jnp.zeros((16, ROWS - OWN_VARS * (PIX + 1), HS), F32)
        for j in range(16):
            col = pl.ds(pl.multiple_of(j * COLS + core * HS, HS), HS)
            for v in range(OWN_VARS):
                rows_f[j, v * PIX : (v + 1) * PIX, :] = emb[v, :, col].astype(F32)
            rows_f[j, OWN_VARS * PIX : OWN_VARS * (PIX + 1), :] = bias[:, col].astype(F32)
        for j in range(16):
            tab_out[j % 4, j // 4] = rows_f[j].astype(BF16)
        row = lax.broadcasted_iota(jnp.int32, (ROWS, TOK), 0)
        pix_f[...] = jnp.where(row < OWN_VARS * (PIX + 1), 1.0, 0.0)
        for v in range(OWN_VARS):
            pix_f[v * PIX : (v + 1) * PIX, :] = pix[v].astype(F32)
        for h in range(2):
            pix_f[ROWS - 2 + h : ROWS - 1 + h, :] = query[h * HS : (h + 1) * HS].astype(F32).reshape(1, HS)
        pat[zl, y] = pix_f[...].astype(BF16)
        tab_mid[y] = tab_out[y]

    def start():
        for i in (1, 2, 3):
            send(pat.at[zl, y], pat.at[zl, y], "pz", "pz", at_var(mod4(zl + i), y))
        for i in (1, 3, 2):
            y_ = mod4(y + i)
            send(tab_out.at[y_], tab_mid.at[y], "ty", "ty", at_var(zl, y_))

    def points_y():
        recv(pat.at[0:3, 0], "pz")
        for i in (1, 3, 2):
            send(pat.at[:, y], pat.at[:, y], "py", "py", at_var(zl, mod4(y + i)))

    def table_z():
        recv(tab_mid.at[0:3], "ty")
        for step in (1, -1, 2 - 4 * core):
            send(tab_mid.at[:, x], tab.at[core, x, zl], "tz", "tz", at_z(step))
        tab[core, x, zl] = tab_mid[:, x]

    def table_x():
        recv(tab.at[core, x, 0:3], "tz")
        for b in (1, -1):
            send(tab.at[core, x], tab.at[core, x], "tx", ("tx", -b % 4), at_seq(0, b, core))
        send(tab.at[core, x], tab.at[core, x], "ts", ("ts", 0), sibling)

    def table_swap(b):
        place = tab.at[core, mod4(x + b)]
        recv(place, ("tx", b % 4))
        if b != 2:
            part = place.at[pl.ds(0 if b == -1 else 2, 2)]
            send(part, part, "tx", ("tx", 2), at_seq(0, -b, core))
        send(place, place, "ts", ("ts", b % 4), sibling)

    def aggregate(b):
        quarter = mod4(x + b)
        if b == 0:
            recv(pat.at[0:3], "py")
            locals_[3].wait()
            for ref, dim in ((collect, 1), (expand, 0)):
                which, real = block_of(lax.broadcasted_iota(jnp.int32, ref.shape, dim))
                own = (which == lax.broadcasted_iota(jnp.int32, ref.shape, 1 - dim)) & real
                ref[...] = jnp.where(own, 1.0, 0.0).astype(BF16)
        recv(tab.at[other, quarter], ("ts", b % 4))
        points_f = pat[...].reshape(DEPTH, TOK).astype(F32)
        twice = jnp.concatenate([points_f, points_f], axis=1)
        tables = [tab[h, quarter].reshape(DEPTH, HS) for h in range(2)]
        queries = pat[quarter, y].astype(F32)
        shares = []
        for h in range(2):
            query_f = queries[ROWS - 2 + h : ROWS - 1 + h, :]
            dots = jnp.sum(tables[h].astype(F32) * query_f, axis=1, keepdims=True)
            shares.append((dots * (1.0 / math.sqrt(HS))) * points_f)
        share = jnp.concatenate(shares, axis=1)
        scores = jnp.zeros((N_VARS, COLS), F32)
        for _ in range(3):
            piece = share.astype(BF16)
            share = share - piece.astype(F32)
            scores = scores + jnp.dot(collect[...], piece, preferred_element_type=F32)
        diagonal = lax.broadcasted_iota(jnp.int32, (N_VARS, N_VARS), 0) == lax.broadcasted_iota(
            jnp.int32, (N_VARS, N_VARS), 1
        )
        keep = jnp.sum(
            jnp.where(diagonal, mask[...].astype(F32).reshape(1, N_VARS), 0.0), axis=1, keepdims=True
        )
        scores = jnp.where(keep > 0.0, scores, -1e30)
        expo = jnp.exp(scores - jnp.max(scores, axis=0, keepdims=True))
        weights = (expo / jnp.sum(expo, axis=0, keepdims=True)).astype(BF16)
        mixed = jnp.dot(expand[...], weights, preferred_element_type=F32) * twice
        high = mixed.astype(BF16)
        low = (mixed - high.astype(F32)).astype(BF16)
        over_rows = (((0,), (0,)), ((), ()))
        merged = []
        for h in range(2):
            cols = slice(h * HS, (h + 1) * HS)
            merged.append(
                lax.dot_general(high[:, cols], tables[h], over_rows, preferred_element_type=F32)
                + lax.dot_general(low[:, cols], tables[h], over_rows, preferred_element_type=F32)
            )
        place = agg.at[quarter * 4 + y]
        place[...] = jnp.concatenate(merged, axis=1).astype(BF16)
        for i in (1, 3, 2):
            send(place, place, "agg", "ay", at_var(zl, mod4(y + i)))

    def layer_norm():
        recv(agg.at[0:12], "ay")
        sums = jnp.zeros((TOK, COLS), F32)
        for v in range(16):
            sums = sums + agg[v].astype(F32)
        mean = jnp.sum(sums, axis=1, keepdims=True) * (1.0 / D)
        sums = jnp.zeros((TOK, COLS), F32)
        for v in range(16):
            centered = agg[v].astype(F32) - mean
            sums = sums + centered * centered
        variance = jnp.sum(sums, axis=1, keepdims=True) * (1.0 / D)
        scale = lax.rsqrt(variance + 1e-05)
        locals_[5].wait()
        for v in range(16):
            cols = slice(v * COLS, (v + 1) * COLS)
            gains = gain[cols].astype(F32).reshape(1, COLS)
            norm[v // 4, :, (v % 4) * COLS : (v % 4 + 1) * COLS] = (
                (agg[v].astype(F32) - mean) * scale * gains
            ).astype(BF16)

    def up_part(a):
        q = mod4(zh + a)
        recv(up.at[q, :, other], ("s", a % 4))
        value = jnp.dot(norm[q], up[q].reshape(1024, FF), preferred_element_type=F32)
        part[...] = value if a == 0 else part[...] + value

    def activate():
        hidden[core] = jax.nn.gelu(part[...], approximate=True).astype(BF16)
        send(hidden.at[core], hidden.at[core], "h", "h", sibling)

    def halves(a):
        n = 2 if a == 2 else 1
        return [slice(i * TOK // n, (i + 1) * TOK // n) for i in range(n)]

    def down_part(a, b):
        if a == 0 and b == 0:
            recv(hidden.at[other], "h")
        q, y_ = mod4(zh + a), mod4(x + b)
        away = mod4(y_ - y)
        value = jnp.dot(hidden[...].reshape(2 * TOK, FF), down[q, y_], preferred_element_type=F32)
        term[a % 4, b % 4] = value.astype(BF16).reshape(2, TOK, HS)

        def deliver(core_):
            for half in halves(a):
                src, dst = term.at[a % 4, b % 4, core_, half], got_y.at[a % 4, away * 2 + core, half]
                send(src, dst, "ry", ("ry", a % 4, half.start), (zl * 4 + y_, zh * 8 + x * 2 + core_))

        deliver(other)

        @pl.when(away == 0)
        def _():
            own_sum[a % 4] = term[a % 4, b % 4, core].astype(F32)

        @pl.when(away != 0)
        def _():
            deliver(core)

    def down_sum(a, number=0):
        a, half = a % 4, halves(a)[number]
        q = mod4(zh + a)
        away = mod4(zl - q)
        recv(got_y.at[a, 0:7, half], ("ry", a, half.start))
        for core_ in (core, other):
            cols = pl.ds(pl.multiple_of(core_ * HS, HS), HS)
            value = own_sum[a, half] if core_ is core else got_y[a, other, half].astype(F32)
            for i in (1, 2, 3):
                value = value + got_y[a, i * 2 + core_, half].astype(F32)

            @pl.when(away == 0)
            def _():
                total[half, cols] = value

            summed[a, half, cols] = value.astype(BF16)

        @pl.when(away != 0)
        def _():
            send(summed.at[a, half], got_z.at[away, half], "rz", "rz", at_var(q, y))

    def all_sent():
        for m in (0, 1):
            sent(up.at[0, 0:3, 0], ("z", m))
            sent(up.at[0:3, :, 0], ("x", m))
        sent(up.at[0:2], "s")
        sent(hidden.at[0], "h")
        sent(pat.at[0, 0:3], "pz")
        sent(pat.at[0:3], "py")
        sent(tab_mid.at[0:3], "tz")
        sent(tab_mid.at[0:3], "ty")
        sent(tab.at[0, 0:3], "tx")
        sent(tab.at[0], "ts")
        sent(agg.at[0:12], "agg")

    def finish():
        result = agg[var].astype(F32) + total[...]
        recv(got_z.at[1:4], "rz")
        for i in (1, 2, 3):
            result = result + got_z[i].astype(F32)
        out[...] = result.astype(BF16)
        sent(got_y.at[:, 0:7], "ry")
        sent(got_z.at[0:3], "rz")

    steps = {
        "pack": pack,
        "start": start,
        "z0": lambda i: z_first(0, i),
        "x0": x_first,
        "z1": lambda i: z_first(1, i),
        "Z": z_piece,
        "Z2": z_far,
        "X": x_piece,
        "XR": x_rest,
        "S": swap,
        "py": points_y,
        "tz": table_z,
        "tx": table_x,
        "tsib": table_swap,
        "agg": aggregate,
        "ln": layer_norm,
        "up": up_part,
        "hid": activate,
        "dp": down_part,
        "sent": all_sent,
        "ds": down_sum,
        "fin": finish,
    }
    for name, *rest in ORDER:
        steps[name](*rest)
    assert len(keys) <= N_RECV and len(groups) <= N_SENT


def shards(pixels, w_embed, var_embed, var_mask, agg_query, ln_gain, w_up, w_down):
    vmem = pltpu.VMEM
    return pl.pallas_call(
        kernel,
        out_shape=jax.ShapeDtypeStruct((TOK, COLS), BF16),
        in_specs=[pl.BlockSpec(memory_space=pl.ANY)] * 8,
        out_specs=pl.BlockSpec(memory_space=pltpu.VMEM),
        scratch_shapes=[
            vmem((OWN_VARS, PIX, TOK), BF16),
            vmem((OWN_VARS, PIX, D), BF16),
            vmem((OWN_VARS, D), BF16),
            vmem((N_VARS,), jnp.int32),
            vmem((COLS,), BF16),
            vmem((D,), BF16),
            vmem((16, ROWS, HS), F32),
            vmem((ROWS, TOK), F32),
            vmem((4, 4, ROWS, HS), BF16),
            vmem((4, 4, ROWS, HS), BF16),
            vmem((2, 4, 4, 4, ROWS, HS), BF16),
            vmem((N_VARS, DEPTH), BF16),
            vmem((DEPTH, N_VARS), BF16),
            vmem((4, 4, ROWS, TOK), BF16),
            vmem((16, TOK, COLS), BF16),
            vmem((4, TOK, 1024), BF16),
            vmem((4, 4, 2, 128, FF), BF16),
            vmem((4, 4, FF, HS), BF16),
            vmem((4, TOK, HS), F32),
            vmem((4, 4, 2, TOK, HS), BF16),
            vmem((4, 8, TOK, HS), BF16),
            vmem((4, TOK, COLS), BF16),
            vmem((4, TOK, COLS), BF16),
            vmem((2, TOK, FF), BF16),
            vmem((TOK, FF), F32),
            vmem((TOK, COLS), F32),
            pltpu.SemaphoreType.DMA((8,)),
            pltpu.SemaphoreType.DMA((N_SENT,)),
            pltpu.SemaphoreType.DMA((N_RECV,)),
        ],
        compiler_params=pltpu.CompilerParams(
            collective_id=0, has_side_effects=True, vmem_limit_bytes=56 * 1024 * 1024
        ),
    )(pixels, w_embed, var_embed, var_mask, agg_query, ln_gain, w_up, w_down)


def solution(mesh):
    return jax.shard_map(
        shards,
        mesh=mesh,
        in_specs=(
            P("var", None, "seq"),
            P("var", None, None),
            P("var", None),
            P(),
            P("var"),
            P(),
            P("seq", "var"),
            P("var", "seq"),
        ),
        out_specs=P("seq", "var"),
        check_vma=False,
    )
```

```python
import math

import jax
import jax.numpy as jnp
from jax import lax
from jax.experimental import pallas as pl
from jax.experimental.pallas import tpu as pltpu
from jax.sharding import PartitionSpec as P

MESH = pl.DeviceIdType.MESH
F32, BF16 = jnp.float32, jnp.bfloat16
PIX, HS = 4, 128
N_VARS = 96
OWN_VARS = 6
ROWS = 32
DEPTH = 16 * ROWS
TOK, COLS, D, FF = 128, 256, 4096, 512
N_SENT, N_RECV = 15, 99
SPLIT = (4, 4)
SPLIT_NEAR = (2, 2)
ORDER = (
    ("x0", 0), ("z0", 0), ("z0", 1), ("start",), ("x0", 1), ("tz",), ("z0", 2), ("X", 0, 0, 1, 1),
    ("X", 1, 0, -1, 0), ("Z", 0, 1, 3), ("py",), ("z0", 3), ("Z", 0, -1, 0), ("X", 1, 0, 1, 1), ("tx",),
    ("X", 0, 0, -1, 0), ("XR", 0, 0, 1), ("Z", 0, -1, 1), ("Z", 0, 1, 2), ("X", 0, 1, 1, 3), ("agg", 0),
    ("XR", 1, 0, 1), ("z1", 0), ("Z", 0, 1, 1), ("tsib", 1), ("tsib", -1), ("Z", 0, -1, 3), ("X", 0, -1, -1, 0),
    ("agg", -1), ("Z", 0, -1, 2), ("XR", 0, 0, -1), ("X", 0, -1, -1, 1), ("z1", 1), ("Z", 0, 1, 0), ("z1", 2),
    ("X", 0, 1, -1, 1), ("agg", 1), ("tsib", 2), ("Z2", 0, 1), ("z1", 3), ("X", 0, 1, 1, 2), ("Z2", 0, 0), ("agg", 2),
    ("XR", 0, 0, 2), ("X", 0, -1, 1, 3), ("Z", 1, 1, 3), ("X", 0, 1, -1, 0), ("S", -1, 0), ("X", 0, -1, 1, 2),
    ("X", 0, 2, -1, 0), ("X", 0, 2, 1, 3), ("X", 0, 2, -1, 1), ("S", 1, 0), ("X", 0, 2, 1, 2), ("Z", 1, 1, 1),
    ("XR", 0, 1, -1), ("XR", 1, 0, -1), ("Z", 1, -1, 0), ("ln",), ("Z", 1, -1, 1), ("XR", 1, 0, 2), ("XR", 0, 2, 1),
    ("S", 2, 0), ("XR", 0, 1, 2), ("XR", 0, -1, -1), ("XR", 0, -1, 1), ("Z", 1, 1, 2), ("XR", 0, 2, 2),
    ("Z", 1, -1, 2), ("XR", 0, 1, 1), ("XR", 0, 2, -1), ("Z", 1, -1, 3), ("up", 0), ("Z", 1, 1, 0), ("XR", 0, -1, 2),
    ("up", 1), ("up", 2), ("up", -1), ("hid",), ("X", 1, -1, -1, 1), ("X", 1, 1, 1, 3), ("Z2", 1, 0), ("dp", 0, 0),
    ("X", 1, -1, -1, 0), ("X", 1, 1, -1, 1), ("X", 1, -1, 1, 2), ("dp", -1, 0), ("X", 1, -1, 1, 3), ("dp", 0, 2),
    ("dp", 0, 1), ("dp", 1, 0), ("Z2", 1, 1), ("X", 1, 1, -1, 0), ("X", 1, 1, 1, 2), ("dp", 2, 0), ("dp", 0, -1),
    ("XR", 1, -1, -1), ("XR", 1, -1, 1), ("X", 1, 2, 1, 3), ("X", 1, 2, -1, 0), ("XR", 1, 1, -1), ("XR", 1, 1, 1),
    ("dp", -1, 1), ("dp", -1, -1), ("XR", 1, -1, 2), ("dp", -1, 2), ("dp", 1, 1), ("X", 1, 2, -1, 1),
    ("X", 1, 2, 1, 2), ("dp", 1, -1), ("XR", 1, 2, -1), ("XR", 1, 1, 2), ("dp", 1, 2), ("dp", 2, -1), ("XR", 1, 2, 1),
    ("XR", 1, 2, 2), ("ds", 0), ("dp", 2, 2), ("dp", 2, 1), ("ds", -1), ("ds", 1), ("ds", 2, 0), ("sent",),
    ("ds", 2, 1), ("fin",),
)


def block_of(iota):
    owner, row = iota // ROWS, iota % ROWS
    local = jnp.where(row < OWN_VARS * PIX, row // PIX, row - OWN_VARS * PIX)
    return owner * OWN_VARS + local, row < OWN_VARS * (PIX + 1)


def kernel(
    pix_in, emb_in, bias_in, mask_in, query_in, gain_in, up_in, down_in, out,
    pix, emb, bias, mask, query, gain, rows_f, pix_f,
    tab_out, tab_mid, tab, collect, expand, pat, agg, norm, up, down, own_sum, term, got_y, got_z, summed, hidden, part, total,
    local_sem, send_sem, recv_sem,
):
    var, seq = lax.axis_index("var"), lax.axis_index("seq")
    zl, y = var // 4, lax.rem(var, 4)
    zh, x, core = seq // 8, lax.rem(seq // 2, 4), lax.rem(seq, 2)
    z = zh * 4 + zl
    other = 1 - core

    def mod4(v):
        return lax.rem(v + 4, 4)

    def at_var(zl_, y_):
        return (zl_ * 4 + y_, seq)

    def at_seq(a, b, core_):
        return (var, mod4(zh + a) * 8 + mod4(x + b) * 2 + core_)

    def at_z(d):
        z_ = lax.rem(z + d + 16, 16)
        return (lax.rem(z_, 4) * 4 + y, (z_ // 4) * 8 + x * 2 + core)

    sibling = at_seq(0, 0, other)

    barrier = pltpu.get_barrier_semaphore()
    peers = [at_z(1), at_z(-1), at_z(2), at_z(-2), sibling]
    peers += [at_var(mod4(zl + i), y) for i in (1, 2, 3)]
    peers += [at_var(zl, mod4(y + i)) for i in (1, 2, 3)]
    peers += [at_seq(1, 0, core), at_seq(-1, 0, core)]
    peers += [at_seq(0, i, core) for i in (1, 3)]
    for peer in peers:
        pl.semaphore_signal(barrier, inc=1, device_id=peer, device_id_type=MESH)

    locals_ = []
    for i, (src, dst) in enumerate(
        (
            (pix_in, pix),
            (emb_in, emb),
            (bias_in, bias),
            (mask_in, mask),
            (query_in, query),
            (gain_in, gain),
            (up_in, up.at[zh, x, core]),
            (down_in, down.at[zh, x]),
        )
    ):
        locals_.append(pltpu.make_async_copy(src, dst, local_sem.at[i]))
        locals_[-1].start()

    groups, keys = {}, {}

    def sem_of(key):
        return keys.setdefault(key, len(keys))

    def copy_of(src, dst, group, key, device):
        return pltpu.make_async_remote_copy(
            src_ref=src,
            dst_ref=dst,
            send_sem=send_sem.at[groups.setdefault(group, len(groups))],
            recv_sem=recv_sem.at[sem_of(key)],
            device_id=device,
            device_id_type=MESH,
        )

    def send(src, dst, group, key, device):
        copy_of(src, dst, group, key, device).start()

    def recv(view, key):
        copy_of(view, view, next(iter(groups)), key, sibling).wait_recv()

    def sent(view, group):
        copy_of(view, view, group, next(iter(keys)), sibling).wait_send()


    def pieces(m, a):
        return (SPLIT if a % 4 else SPLIT_NEAR)[m]

    def rows_of(m, a, p, count=1):
        n = (HS, FF)[m] // pieces(m, a)
        return pl.ds(p * n, n * count)

    def block(m, a, b, core_):
        if m == 0:
            return up.at[mod4(zh + a), mod4(x + b), core_]
        return down.at[mod4(zh + a), mod4(x + b)]

    def piece(m, a, b, p, count=1):
        if m == 0:
            return block(m, a, b, core).at[rows_of(m, a, p, count)]
        return down.at[mod4(zh + a), mod4(x + b), rows_of(m, a, p, count)]

    def z_key(m, a, p):
        return ("z", m, a % 4, p)

    def x_key(m, a, b, p):
        n = pieces(m, a)
        alone = (b % 4 == 3 and p < n // 2) or (b % 4 == 1 and p >= n // 2)
        return ("x", m, a % 4, b % 4, p if alone else "rest")

    def z_send(m, a, p, way):
        step = {"z+": 1, "z-": -1}[way]
        if a == 0:
            rows = rows_of(m, 1, p)
            if m == 0:
                src = dst = up.at[zh, x, core].at[rows]
            else:
                src = dst = down.at[zh, x, rows]
        else:
            src = dst = piece(m, a, 0, p)
        send(src, dst, ("z", m), z_key(m, a - step, p), at_seq(step, 0, core))

    def x_send(m, a, b, p, way):
        step = {"x+": 1, "x-": -1}[way]
        src = dst = piece(m, a, b, p)
        send(src, dst, ("x", m), x_key(m, a, b - step, p), at_seq(0, step, core))

    def swap(a, b):
        place = block(0, a, b, core)
        send(place, place, "s", ("s", a % 4), sibling)

    def z_first(m, i):
        z_send(m, 0, i, "z+")
        z_send(m, 0, pieces(m, 1) - 1 - i, "z-")

    def x_first(m):
        n = pieces(m, 0)
        for i in range(n):
            x_send(m, 0, 0, i, "x+")
            x_send(m, 0, 0, n - 1 - i, "x-")
        if m == 0:
            swap(0, 0)

    def z_piece(m, a, p):
        n = pieces(m, a)
        recv(piece(m, a, 0, p), z_key(m, a, p))
        if a == -1 and p < n // 2:
            z_send(m, a, p, "z+")
        if a == 1 and p >= n // 2:
            z_send(m, a, p, "z-")
        x_send(m, a, 0, p, "x+")
        x_send(m, a, 0, p, "x-")

    def z_far(m, low):
        high = pieces(m, 2) - 1 - low
        for p in (low, high):
            recv(piece(m, 2, 0, p), z_key(m, 2, p))
        x_send(m, 2, 0, low, "x+")
        x_send(m, 2, 0, high, "x-")
        x_send(m, 2, 0, high, "x+")
        x_send(m, 2, 0, low, "x-")

    def x_piece(m, a, b, p):
        recv(piece(m, a, b, p), x_key(m, a, b, p))
        x_send(m, a, b, p, "x+" if b == -1 else "x-")

    def x_rest(m, a, b):
        n = pieces(m, a)
        first, count = {-1: (n // 2, n // 2), 1: (0, n // 2), 2: (0, n)}[b]
        recv(piece(m, a, b, first, count), x_key(m, a, b, first))
        if m == 0:
            swap(a, b)

    def pack():
        for i in (0, 1, 2, 4):
            locals_[i].wait()
        rows_f[:, OWN_VARS * (PIX + 1) :, :] = jnp.zeros((16, ROWS - OWN_VARS * (PIX + 1), HS), F32)
        for j in range(16):
            col = pl.ds(pl.multiple_of(j * COLS + core * HS, HS), HS)
            for v in range(OWN_VARS):
                rows_f[j, v * PIX : (v + 1) * PIX, :] = emb[v, :, col].astype(F32)
            rows_f[j, OWN_VARS * PIX : OWN_VARS * (PIX + 1), :] = bias[:, col].astype(F32)
        for j in range(16):
            tab_out[j % 4, j // 4] = rows_f[j].astype(BF16)
        row = lax.broadcasted_iota(jnp.int32, (ROWS, TOK), 0)
        pix_f[...] = jnp.where(row < OWN_VARS * (PIX + 1), 1.0, 0.0)
        for v in range(OWN_VARS):
            pix_f[v * PIX : (v + 1) * PIX, :] = pix[v].astype(F32)
        for h in range(2):
            pix_f[ROWS - 2 + h : ROWS - 1 + h, :] = query[h * HS : (h + 1) * HS].astype(F32).reshape(1, HS)
        pat[zl, y] = pix_f[...].astype(BF16)
        tab_mid[y] = tab_out[y]

    def start():
        for i in (1, 2, 3):
            send(pat.at[zl, y], pat.at[zl, y], "pz", "pz", at_var(mod4(zl + i), y))
        for i in (1, 3, 2):
            y_ = mod4(y + i)
            send(tab_out.at[y_], tab_mid.at[y], "ty", "ty", at_var(zl, y_))

    def points_y():
        recv(pat.at[0:3, 0], "pz")
        for i in (1, 3, 2):
            send(pat.at[:, y], pat.at[:, y], "py", "py", at_var(zl, mod4(y + i)))

    def table_z():
        recv(tab_mid.at[0:3], "ty")
        for step in (1, -1, 2 - 4 * core):
            send(tab_mid.at[:, x], tab.at[core, x, zl], "tz", "tz", at_z(step))
        tab[core, x, zl] = tab_mid[:, x]

    def table_x():
        recv(tab.at[core, x, 0:3], "tz")
        for b in (1, -1):
            send(tab.at[core, x], tab.at[core, x], "tx", ("tx", -b % 4), at_seq(0, b, core))
        send(tab.at[core, x], tab.at[core, x], "ts", ("ts", 0), sibling)

    def table_swap(b):
        place = tab.at[core, mod4(x + b)]
        recv(place, ("tx", b % 4))
        if b != 2:
            part = place.at[pl.ds(0 if b == -1 else 2, 2)]
            send(part, part, "tx", ("tx", 2), at_seq(0, -b, core))
        send(place, place, "ts", ("ts", b % 4), sibling)

    def aggregate(b):
        quarter = mod4(x + b)
        if b == 0:
            recv(pat.at[0:3], "py")
            locals_[3].wait()
        recv(tab.at[other, quarter], ("ts", b % 4))
        points_f = pat[...].reshape(DEPTH, TOK).astype(F32)
        twice = jnp.concatenate([points_f, points_f], axis=1)
        tables = [tab[h, quarter].reshape(DEPTH, HS) for h in range(2)]
        queries = pat[quarter, y].astype(F32)
        shares = []
        for h in range(2):
            query_f = queries[ROWS - 2 + h : ROWS - 1 + h, :]
            dots = jnp.sum(tables[h].astype(F32) * query_f, axis=1, keepdims=True)
            shares.append((dots * (1.0 / math.sqrt(HS))) * points_f)
        share = jnp.concatenate(shares, axis=1)
        scores = jnp.zeros((N_VARS, COLS), F32)
        for _ in range(3):
            piece = share.astype(BF16)
            share = share - piece.astype(F32)
            scores = scores + jnp.dot(collect[...], piece, preferred_element_type=F32)
        diagonal = lax.broadcasted_iota(jnp.int32, (N_VARS, N_VARS), 0) == lax.broadcasted_iota(
            jnp.int32, (N_VARS, N_VARS), 1
        )
        keep = jnp.sum(
            jnp.where(diagonal, mask[...].astype(F32).reshape(1, N_VARS), 0.0), axis=1, keepdims=True
        )
        scores = jnp.where(keep > 0.0, scores, -1e30)
        expo = jnp.exp(scores - jnp.max(scores, axis=0, keepdims=True))
        weights = (expo / jnp.sum(expo, axis=0, keepdims=True)).astype(BF16)
        mixed = jnp.dot(expand[...], weights, preferred_element_type=F32) * twice
        high = mixed.astype(BF16)
        low = (mixed - high.astype(F32)).astype(BF16)
        over_rows = (((0,), (0,)), ((), ()))
        merged = []
        for h in range(2):
            cols = slice(h * HS, (h + 1) * HS)
            merged.append(
                lax.dot_general(high[:, cols], tables[h], over_rows, preferred_element_type=F32)
                + lax.dot_general(low[:, cols], tables[h], over_rows, preferred_element_type=F32)
            )
        place = agg.at[quarter * 4 + y]
        place[...] = jnp.concatenate(merged, axis=1).astype(BF16)
        for i in (1, 3, 2):
            send(place, place, "agg", "ay", at_var(zl, mod4(y + i)))

    def layer_norm():
        recv(agg.at[0:12], "ay")
        sums = jnp.zeros((TOK, COLS), F32)
        for v in range(16):
            sums = sums + agg[v].astype(F32)
        mean = jnp.sum(sums, axis=1, keepdims=True) * (1.0 / D)
        sums = jnp.zeros((TOK, COLS), F32)
        for v in range(16):
            centered = agg[v].astype(F32) - mean
            sums = sums + centered * centered
        variance = jnp.sum(sums, axis=1, keepdims=True) * (1.0 / D)
        scale = lax.rsqrt(variance + 1e-05)
        locals_[5].wait()
        for v in range(16):
            cols = slice(v * COLS, (v + 1) * COLS)
            gains = gain[cols].astype(F32).reshape(1, COLS)
            norm[v // 4, :, (v % 4) * COLS : (v % 4 + 1) * COLS] = (
                (agg[v].astype(F32) - mean) * scale * gains
            ).astype(BF16)

    def up_part(a):
        q = mod4(zh + a)
        recv(up.at[q, :, other], ("s", a % 4))
        value = jnp.dot(norm[q], up[q].reshape(1024, FF), preferred_element_type=F32)
        part[...] = value if a == 0 else part[...] + value

    def activate():
        hidden[core] = jax.nn.gelu(part[...], approximate=True).astype(BF16)
        send(hidden.at[core], hidden.at[core], "h", "h", sibling)

    def halves(a):
        n = 2 if a == 2 else 1
        return [slice(i * TOK // n, (i + 1) * TOK // n) for i in range(n)]

    def down_part(a, b):
        if a == 0 and b == 0:
            recv(hidden.at[other], "h")
        q, y_ = mod4(zh + a), mod4(x + b)
        away = mod4(y_ - y)
        value = jnp.dot(hidden[...].reshape(2 * TOK, FF), down[q, y_], preferred_element_type=F32)
        term[a % 4, b % 4] = value.astype(BF16).reshape(2, TOK, HS)

        def deliver(core_):
            for half in halves(a):
                src, dst = term.at[a % 4, b % 4, core_, half], got_y.at[a % 4, away * 2 + core, half]
                send(src, dst, "ry", ("ry", a % 4, half.start), (zl * 4 + y_, zh * 8 + x * 2 + core_))

        deliver(other)

        @pl.when(away == 0)
        def _():
            own_sum[a % 4] = term[a % 4, b % 4, core].astype(F32)

        @pl.when(away != 0)
        def _():
            deliver(core)

    def down_sum(a, number=0):
        a, half = a % 4, halves(a)[number]
        q = mod4(zh + a)
        away = mod4(zl - q)
        recv(got_y.at[a, 0:7, half], ("ry", a, half.start))
        for core_ in (core, other):
            cols = pl.ds(pl.multiple_of(core_ * HS, HS), HS)
            value = own_sum[a, half] if core_ is core else got_y[a, other, half].astype(F32)
            for i in (1, 2, 3):
                value = value + got_y[a, i * 2 + core_, half].astype(F32)

            @pl.when(away == 0)
            def _():
                total[half, cols] = value

            summed[a, half, cols] = value.astype(BF16)

        @pl.when(away != 0)
        def _():
            send(summed.at[a, half], got_z.at[away, half], "rz", "rz", at_var(q, y))

    def all_sent():
        for m in (0, 1):
            sent(up.at[0, 0:3, 0], ("z", m))
            sent(up.at[0:3, :, 0], ("x", m))
        sent(up.at[0:2], "s")
        sent(hidden.at[0], "h")
        sent(pat.at[0, 0:3], "pz")
        sent(pat.at[0:3], "py")
        sent(tab_mid.at[0:3], "tz")
        sent(tab_mid.at[0:3], "ty")
        sent(tab.at[0, 0:3], "tx")
        sent(tab.at[0], "ts")
        sent(agg.at[0:12], "agg")

    def finish():
        result = agg[var].astype(F32) + total[...]
        recv(got_z.at[1:4], "rz")
        for i in (1, 2, 3):
            result = result + got_z[i].astype(F32)
        out[...] = result.astype(BF16)
        sent(got_y.at[:, 0:7], "ry")
        sent(got_z.at[0:3], "rz")

    steps = {
        "pack": pack,
        "start": start,
        "z0": lambda i: z_first(0, i),
        "x0": x_first,
        "z1": lambda i: z_first(1, i),
        "Z": z_piece,
        "Z2": z_far,
        "X": x_piece,
        "XR": x_rest,
        "S": swap,
        "py": points_y,
        "tz": table_z,
        "tx": table_x,
        "tsib": table_swap,
        "agg": aggregate,
        "ln": layer_norm,
        "up": up_part,
        "hid": activate,
        "dp": down_part,
        "sent": all_sent,
        "ds": down_sum,
        "fin": finish,
    }
    pack()
    for ref, dim in ((collect, 1), (expand, 0)):
        which, real = block_of(lax.broadcasted_iota(jnp.int32, ref.shape, dim))
        own = (which == lax.broadcasted_iota(jnp.int32, ref.shape, 1 - dim)) & real
        ref[...] = jnp.where(own, 1.0, 0.0).astype(BF16)
    pl.semaphore_wait(barrier, len(peers))
    for i in (6, 7):
        locals_[i].wait()
    for name, *rest in ORDER:
        steps[name](*rest)
    assert len(keys) <= N_RECV and len(groups) <= N_SENT


def shards(pixels, w_embed, var_embed, var_mask, agg_query, ln_gain, w_up, w_down):
    vmem = pltpu.VMEM
    return pl.pallas_call(
        kernel,
        out_shape=jax.ShapeDtypeStruct((TOK, COLS), BF16),
        in_specs=[pl.BlockSpec(memory_space=pl.ANY)] * 8,
        out_specs=pl.BlockSpec(memory_space=pltpu.VMEM),
        scratch_shapes=[
            vmem((OWN_VARS, PIX, TOK), BF16),
            vmem((OWN_VARS, PIX, D), BF16),
            vmem((OWN_VARS, D), BF16),
            vmem((N_VARS,), jnp.int32),
            vmem((COLS,), BF16),
            vmem((D,), BF16),
            vmem((16, ROWS, HS), F32),
            vmem((ROWS, TOK), F32),
            vmem((4, 4, ROWS, HS), BF16),
            vmem((4, 4, ROWS, HS), BF16),
            vmem((2, 4, 4, 4, ROWS, HS), BF16),
            vmem((N_VARS, DEPTH), BF16),
            vmem((DEPTH, N_VARS), BF16),
            vmem((4, 4, ROWS, TOK), BF16),
            vmem((16, TOK, COLS), BF16),
            vmem((4, TOK, 1024), BF16),
            vmem((4, 4, 2, 128, FF), BF16),
            vmem((4, 4, FF, HS), BF16),
            vmem((4, TOK, HS), F32),
            vmem((4, 4, 2, TOK, HS), BF16),
            vmem((4, 8, TOK, HS), BF16),
            vmem((4, TOK, COLS), BF16),
            vmem((4, TOK, COLS), BF16),
            vmem((2, TOK, FF), BF16),
            vmem((TOK, FF), F32),
            vmem((TOK, COLS), F32),
            pltpu.SemaphoreType.DMA((8,)),
            pltpu.SemaphoreType.DMA((N_SENT,)),
            pltpu.SemaphoreType.DMA((N_RECV,)),
        ],
        compiler_params=pltpu.CompilerParams(
            collective_id=0, has_side_effects=True, vmem_limit_bytes=56 * 1024 * 1024
        ),
    )(pixels, w_embed, var_embed, var_mask, agg_query, ln_gain, w_up, w_down)


def solution(mesh):
    return jax.shard_map(
        shards,
        mesh=mesh,
        in_specs=(
            P("var", None, "seq"),
            P("var", None, None),
            P("var", None),
            P(),
            P("var"),
            P(),
            P("seq", "var"),
            P("var", "seq"),
        ),
        out_specs=P("seq", "var"),
        check_vma=False,
    )
```
